32 devices in a mesh: rad: 8 (over y, x, core), az: 4 (over z).
Axes of the slice: x: 2, y: 2, z: 4, core: 2. Of those that a mesh axis runs over, the one named last changes fastest.
Arguments:
- fields: float32 [5, 48, 8, 1024], P(None, 'rad', None, 'az'), may hold values from -0.9 to 4, as said below
- shifts: int32 [48], P('rad'), may hold values from 0 to 768, as said below
Outputs:
- advanced: float32 [5, 48, 8, 1024], P(None, 'rad', None, 'az')
The draws below stay inside these ranges and needn't reach their ends.
Inputs may be any that keep to these rules, and one draw needn't show every extreme that they name: `fields`: components 0 (density) and 4 (pressure) lie in 2.0 to 4.0; components 1 to 3 (velocities) lie in -0.9 to 0.9. The first radius row shifts by 768 cells and the last one by 0.
All inputs are finite; a program needn't handle non-finite values.
Results may differ from the reference program's by a relative error of at most 0.0003.
Values sent between devices are 32-bit elements; how exact they have to be, the bound alone decides.
A program may use at most 64 MiB of HBM per device.

```python
import math
import jax
import jax.numpy as jnp
from jax import lax

CR = 6
CTH = 8
CPHI = 256
STEPS = 1
NR = 48
NPHI = 1024
N_RAD = 8


def wave_field(key, periods, amplitude):
    phases = jax.random.uniform(key, (len(periods),), jnp.float32, 0.0, 2.0 * math.pi)
    radius = jnp.arange(NR, dtype=jnp.int32)[:, None, None]
    polar_index = jnp.arange(CTH, dtype=jnp.int32)[None, :, None]
    azimuth = jnp.arange(NPHI, dtype=jnp.int32)[None, None, :]
    layers = []
    for component in range(len(periods)):
        radial_period, polar_period, azimuth_period = periods[component]
        turning = (radius % radial_period).astype(jnp.float32) / radial_period
        turning = turning + (polar_index % polar_period).astype(jnp.float32) / polar_period
        turning = turning + (azimuth % azimuth_period).astype(jnp.float32) / azimuth_period
        layers.append(amplitude[component] * jnp.sin(2.0 * math.pi * turning + phases[component]))
    return jnp.stack(layers)


def draw_fields(key, part):
    split_keys = jax.random.split(jax.random.fold_in(key, 11), 2)
    grid_shape = (5, NR, CTH, NPHI)
    centre_values = jnp.array([3.0, 0.0, 0.0, 0.0, 3.0], dtype=jnp.float32)[:, None, None, None]
    smooth = wave_field(split_keys[1], [(10, 8, 12), (14, 6, 16), (9, 7, 11), (12, 5, 13), (11, 9, 10)], [0.55, 0.5, 0.5, 0.5, 0.55])
    rough = jnp.clip(0.15 * jax.random.normal(split_keys[0], grid_shape, jnp.float32), -0.4, 0.4)
    return (centre_values + smooth + rough).astype(jnp.float32)


def draw_shifts(key, part):
    row_index = jnp.arange(NR, dtype=jnp.int32)
    profile = 3 * CPHI * NR // (NR + 3 * row_index)
    jitter = jax.random.randint(jax.random.fold_in(key, 23), (NR,), 0, CPHI // 2 + 1)
    counts = jnp.clip(profile - jitter, 0, 3 * CPHI)
    counts = jnp.where(row_index == 0, 3 * CPHI, counts)
    return jnp.where(row_index == NR - 1, 0, counts).astype(jnp.int32)


def setup_inputs(seed: int = 0) -> dict:
    seeds = jax.random.split(jax.random.key(seed), 3)
    fields = draw_fields(jax.random.fold_in(seeds[2], 71), 0)
    shifts = draw_shifts(jax.random.fold_in(seeds[2], 71), 0)
    return dict(fields=fields, shifts=shifts)


ADIABATIC = 1.4
COURANT_RADIAL = 0.09
COURANT_POLAR = 0.08
COURANT_AZIMUTH = 0.18

def cut_along(values, first_cell, finish, along):
    return lax.slice_in_dim(values, first_cell, finish, axis=along)

def edge_states(values, along):
    length = values.shape[along]
    before = cut_along(values, 0, length - 3, along)
    centre = cut_along(values, 1, length - 2, along)
    follow = cut_along(values, 2, length - 1, along)
    beyond = cut_along(values, 3, length, along)
    interface = 7.0 / 12.0 * (centre + follow) - 1.0 / 12.0 * (before + beyond)
    interface = jnp.clip(interface, jnp.minimum(centre, follow), jnp.maximum(centre, follow))
    count = length - 3
    left_edge = cut_along(interface, 0, count - 1, along)
    right_edge = cut_along(interface, 1, count, along)
    middle_cell = cut_along(values, 2, length - 2, along)
    no_slope = (right_edge - middle_cell) * (middle_cell - left_edge) <= 0.0
    left_edge = jnp.where(no_slope, middle_cell, left_edge)
    right_edge = jnp.where(no_slope, middle_cell, right_edge)
    spread = right_edge - left_edge
    middle = middle_cell - 0.5 * (left_edge + right_edge)
    new_left = jnp.where(spread * middle > spread * spread / 6.0, 3.0 * middle_cell - 2.0 * right_edge, left_edge)
    new_right = jnp.where(spread * middle < -spread * spread / 6.0, 3.0 * middle_cell - 2.0 * left_edge, right_edge)
    return (new_left, new_right)

def primitive_parts(state, normal):
    density = state[0]
    pressure = state[4]
    normal_speed = state[normal]
    squared = state[1] * state[1] + state[2] * state[2] + state[3] * state[3]
    energy = pressure / (ADIABATIC - 1.0) + 0.5 * density * squared
    sound_speed = jnp.sqrt(ADIABATIC * pressure / density)
    conserved = [density, density * state[1], density * state[2], density * state[3], energy]
    flux_list = [plain_term * normal_speed for plain_term in conserved]
    flux_list[normal] = flux_list[normal] + pressure
    flux_list[4] = flux_list[4] + pressure * normal_speed
    return (density, pressure, normal_speed, energy, sound_speed, conserved, flux_list)

def star_flux(state, parts, wave_speed, contact, normal):
    density, pressure, normal_speed, energy, sound_speed, conserved, flux_list = parts
    factor = density * (wave_speed - normal_speed) / (wave_speed - contact)
    star_energy = factor * (energy / density + (contact - normal_speed) * (contact + pressure / (density * (wave_speed - normal_speed))))
    star_state = [factor, factor * state[1], factor * state[2], factor * state[3], star_energy]
    star_state[normal] = factor * contact
    return [flux_term + wave_speed * (star_term - plain_term) for flux_term, star_term, plain_term in zip(flux_list, star_state, conserved)]

def riemann_flux(left_state, right_state, normal):
    left_parts = primitive_parts(left_state, normal)
    right_parts = primitive_parts(right_state, normal)
    slow_wave = jnp.minimum(left_parts[2] - left_parts[4], right_parts[2] - right_parts[4])
    fast_wave = jnp.maximum(left_parts[2] + left_parts[4], right_parts[2] + right_parts[4])
    mass_left = left_parts[0] * (left_parts[2] - slow_wave)
    mass_right = right_parts[0] * (fast_wave - right_parts[2])
    contact = (mass_left * left_parts[2] + mass_right * right_parts[2] + left_parts[1] - right_parts[1]) / (mass_left + mass_right)
    star_left = star_flux(left_state, left_parts, slow_wave, contact, normal)
    star_right = star_flux(right_state, right_parts, fast_wave, contact, normal)
    merged = []
    for flux_left, inner_left, inner_right, flux_right in zip(left_parts[6], star_left, star_right, right_parts[6]):
        merged.append(jnp.where(slow_wave >= 0.0, flux_left, jnp.where(contact >= 0.0, inner_left, jnp.where(fast_wave > 0.0, inner_right, flux_right))))
    return jnp.stack(merged)

def flux_difference(window, along, normal):
    left_edge, right_edge = edge_states(window, along)
    cell_total = left_edge.shape[along]
    from_left = cut_along(right_edge, 0, cell_total - 1, along)
    from_right = cut_along(left_edge, 1, cell_total, along)
    flux_all = riemann_flux(from_left, from_right, normal)
    faces = flux_all.shape[along]
    return cut_along(flux_all, 1, faces, along) - cut_along(flux_all, 0, faces - 1, along)

def tendency(window, courant_rows):
    padded = jnp.pad(window, ((0, 0), (0, 0), (3, 3), (0, 0)), mode='edge')
    radial_term = flux_difference(padded[:, :, 3:-3, 3:-3], 1, 1)
    polar_term = flux_difference(padded[:, 3:-3, :, 3:-3], 2, 2)
    azimuth_term = flux_difference(padded[:, 3:-3, 3:-3, :], 3, 3)
    return -(COURANT_RADIAL * radial_term + COURANT_POLAR * polar_term + courant_rows[None, :, None, None] * azimuth_term)

def courant_profile(row_index, total_rows):
    return COURANT_AZIMUTH / (1.0 + (row_index + 0.5) / total_rows)

def to_conserved(primitive):
    density = primitive[0]
    squared = primitive[1] * primitive[1] + primitive[2] * primitive[2] + primitive[3] * primitive[3]
    energy = primitive[4] / (ADIABATIC - 1.0) + 0.5 * density * squared
    return jnp.stack([density, density * primitive[1], density * primitive[2], density * primitive[3], energy])

def to_primitive(conserved):
    density = conserved[0]
    velocity = conserved[1:4] / density
    squared = velocity[0] * velocity[0] + velocity[1] * velocity[1] + velocity[2] * velocity[2]
    pressure = (ADIABATIC - 1.0) * (conserved[4] - 0.5 * density * squared)
    return jnp.concatenate([density[None], velocity, pressure[None]])

def section_change(primitive, courant_all):
    padded = jnp.pad(primitive, ((0, 0), (3, 3), (0, 0), (0, 0)), mode='edge')
    padded = jnp.pad(padded, ((0, 0), (0, 0), (0, 0), (3, 3)), mode='wrap')

    def radial_block(block_index):
        window = lax.dynamic_slice_in_dim(padded, block_index * CR, CR + 6, axis=1)
        rows_here = lax.dynamic_slice_in_dim(courant_all, block_index * CR, CR)
        return tendency(window, rows_here)
    pieces = lax.map(radial_block, jnp.arange(N_RAD, dtype=jnp.int32))
    return jnp.moveaxis(pieces, 0, 1).reshape(primitive.shape)

def advect(primitive, shifts):

    def roll_row(one_row, amount):
        return jnp.roll(one_row, amount, axis=2)
    return jax.vmap(roll_row, in_axes=(1, 0), out_axes=1)(primitive, shifts)

def reference(fields, shifts):
    row_index = jnp.arange(NR, dtype=jnp.int32).astype(jnp.float32)
    courant_all = courant_profile(row_index, NR)
    current = fields
    for step_index in range(STEPS):
        initial = to_conserved(current)
        section_one = initial + section_change(current, courant_all)
        section_one_prim = to_primitive(section_one)
        section_two = 0.5 * initial + 0.5 * (section_one + section_change(section_one_prim, courant_all))
        current = advect(to_primitive(section_two), shifts)
    return current
```

```python
import functools

import jax
import jax.numpy as jnp
from jax import lax
from jax.experimental import pallas as pl
from jax.experimental.pallas import tpu as pltpu
from jax.sharding import PartitionSpec as P

ADIABATIC = 1.4
COURANT_RADIAL = 0.09
COURANT_POLAR = 0.08
COURANT_AZIMUTH = 0.18
MESH = pl.DeviceIdType.MESH
LANES = 128
DEEP = 6
SLOT = 8
PER_TILE = LANES // SLOT
REACH = 3


def pack_edges(block_ref, pack_ref, side):
    comps, rows, polar, cells = block_ref.shape
    lane = lax.broadcasted_iota(jnp.int32, (polar, LANES), 1) // SLOT
    start = 0 if side == 0 else cells - LANES
    for tile in range(pack_ref.shape[1]):
        total = jnp.zeros((polar, LANES), jnp.float32)
        for slot in range(PER_TILE):
            plane = tile * PER_TILE + slot
            if plane < comps * rows:
                part = block_ref[plane // rows, plane % rows, :, start : start + LANES]
                amount = (slot * SLOT + (0 if side == 0 else SLOT)) % LANES
                if amount:
                    part = pltpu.roll(part, amount, 1)
                total = jnp.where(lane == slot, part, total)
        pack_ref[side, tile] = total


def halo_kernel(n_rad, n_az, block_ref, low_ref, up_ref, edge_ref, pack_ref, send_sem, recv_sem):
    rad, az = lax.axis_index("rad"), lax.axis_index("az")
    right, left = lax.rem(az + 1, n_az), lax.rem(az + n_az - 1, n_az)
    has = {-1: rad > 0, 1: rad < n_rad - 1}

    def when(step, work):
        if step == 0:
            work()
        else:
            pl.when(has[step])(work)

    barrier = pltpu.get_barrier_semaphore()

    def greet(step):
        def work():
            for column in (left, right) if step == 0 else (az, left, right):
                pl.semaphore_signal(
                    barrier, inc=1, device_id={"rad": rad + step, "az": column}, device_id_type=MESH
                )

        return work

    for step in (0, -1, 1):
        when(step, greet(step))
    inside = jnp.logical_and(has[-1], has[1])
    pl.semaphore_wait(barrier, jnp.where(inside, 8, 5 if n_rad > 1 else 2))

    def radial(step):
        return pltpu.make_async_remote_copy(
            src_ref=block_ref,
            dst_ref=up_ref if step < 0 else low_ref,
            send_sem=send_sem.at[0 if step < 0 else 1],
            recv_sem=recv_sem.at[0 if step < 0 else 1],
            device_id={"rad": rad + step, "az": az},
            device_id_type=MESH,
        )

    def edge(step, side):
        slot = side * 3 + 1 - step
        return pltpu.make_async_remote_copy(
            src_ref=pack_ref.at[side],
            dst_ref=edge_ref.at[slot],
            send_sem=send_sem.at[2 + slot],
            recv_sem=recv_sem.at[2 + slot],
            device_id={"rad": rad + step, "az": left if side == 0 else right},
            device_id_type=MESH,
        )

    for step in (-1, 1):
        when(step, lambda step=step: radial(step).start())
    for side in (0, 1):
        pack_edges(block_ref, pack_ref, side)
        for step in (0, -1, 1):
            when(step, lambda step=step, side=side: edge(step, side).start())
    for side in (0, 1):
        for step in (0, -1, 1):
            when(step, lambda step=step, side=side: edge(step, side).wait_send())
            when(-step, lambda step=step, side=side: edge(step, side).wait_recv())
    for step in (-1, 1):
        when(step, lambda step=step: radial(step).wait_send())
        when(-step, lambda step=step: radial(step).wait_recv())


def interface(before, centre, follow, beyond):
    value = 7.0 / 12.0 * (centre + follow) - 1.0 / 12.0 * (before + beyond)
    return jnp.clip(value, jnp.minimum(centre, follow), jnp.maximum(centre, follow))


def limited(u, left, right):
    flat = (right - u) * (u - left) <= 0.0
    spread = right - left
    middle = u - 0.5 * (left + right)
    product = spread * middle
    sixth = spread * spread * (1.0 / 6.0)
    triple = 3.0 * u
    new_left = jnp.where(flat, u, jnp.where(product > sixth, triple - 2.0 * right, left))
    new_right = jnp.where(flat, u, jnp.where(product < -sixth, triple - 2.0 * left, right))
    return new_left, new_right


def hllc(left, right, normal):
    gas_left, gas_right = ADIABATIC * left[4], ADIABATIC * right[4]
    sound_left = gas_left * lax.rsqrt(gas_left * left[0])
    sound_right = gas_right * lax.rsqrt(gas_right * right[0])
    u_left, u_right = left[normal], right[normal]
    slow = jnp.minimum(u_left - sound_left, u_right - sound_right)
    fast = jnp.maximum(u_left + sound_left, u_right + sound_right)
    mass_left = left[0] * (u_left - slow)
    mass_right = right[0] * (fast - u_right)
    contact = (mass_left * u_left + mass_right * u_right + left[4] - right[4]) / (
        mass_left + mass_right
    )
    supersonic = slow >= 0.0
    from_left = jnp.logical_or(supersonic, contact >= 0.0)
    rho, v1, v2, v3, p = [jnp.where(from_left, a, b) for a, b in zip(left, right)]
    speeds = (None, v1, v2, v3)
    u = speeds[normal]
    wave = jnp.where(from_left, slow, fast)
    star = jnp.logical_and(slow < 0.0, jnp.logical_or(from_left, fast > 0.0))
    energy = p * (1.0 / (ADIABATIC - 1.0)) + 0.5 * rho * (v1 * v1 + v2 * v2 + v3 * v3)
    momentum = rho * u
    relative = wave - u
    mass = rho * relative
    inverse = 1.0 / (wave - contact)
    factor = mass * inverse
    star_energy = inverse * (relative * energy + (contact - u) * (mass * contact + p))
    flux_mass = momentum + jnp.where(star, wave * (factor - rho), 0.0)
    flux_normal = momentum * u + p + jnp.where(star, wave * (factor * contact - momentum), 0.0)
    flux_energy = (energy + p) * u + jnp.where(star, wave * (star_energy - energy), 0.0)
    out = [flux_mass, None, None, None, flux_energy]
    for axis in (1, 2, 3):
        out[axis] = flux_normal if axis == normal else speeds[axis] * flux_mass
    return out


def conserved_of(w):
    energy = w[4] * (1.0 / (ADIABATIC - 1.0)) + 0.5 * w[0] * (
        w[1] * w[1] + w[2] * w[2] + w[3] * w[3]
    )
    return [w[0], w[0] * w[1], w[0] * w[2], w[0] * w[3], energy]


def primitive_of(u):
    inverse = 1.0 / u[0]
    v = [inverse * u[k] for k in (1, 2, 3)]
    squared = v[0] * v[0] + v[1] * v[1] + v[2] * v[2]
    return [u[0]] + v + [(ADIABATIC - 1.0) * (u[4] - 0.5 * u[0] * squared)]


def rolled(x, amount, axis):
    return pltpu.roll(x, amount % x.shape[axis], axis)


def azimuth_difference(w):
    lows, highs = [], []
    for u in w:
        edge = interface(rolled(u, 1, 1), u, rolled(u, -1, 1), rolled(u, -2, 1))
        low, high = limited(u, rolled(edge, 1, 1), edge)
        lows.append(low)
        highs.append(rolled(high, 1, 1))
    flux = hllc(highs, lows, 3)
    return [rolled(f, -1, 1) - f for f in flux]


def polar_difference(w):
    count = w[0].shape[0]
    place = lax.broadcasted_iota(jnp.int32, w[0].shape, 0)
    first, last = place == 0, place == count - 1
    beyond_last = place >= count - 2
    lows, highs = [], []
    for u in w:
        before = jnp.where(first, u, rolled(u, 1, 0))
        follow = jnp.where(last, u, rolled(u, -1, 0))
        beyond = jnp.where(beyond_last, jnp.where(last, u, follow), rolled(u, -2, 0))
        edge = interface(before, u, follow, beyond)
        low, high = limited(u, jnp.where(first, u, rolled(edge, 1, 0)), edge)
        lows.append(low)
        highs.append(jnp.where(first, u, rolled(high, 1, 0)))
    flux = hllc(highs, lows, 2)
    rho, v1, v2, v3, p = w
    momentum = rho * v2
    energy = conserved_of(w)[4]
    outer = [momentum, momentum * v1, momentum * v2 + p, momentum * v3, (energy + p) * v2]
    return [jnp.where(last, o, rolled(f, -1, 0)) - f for f, o in zip(flux, outer)]


def row_of(ref, row, width):
    return [ref[c, row, :, :width] for c in range(5)]


def radial_start(src, cell, width, keep):
    w = [row_of(src, cell + k, width) for k in (-2, -1, 0, 1, 2)]
    for c in range(5):
        below = interface(*(w[k][c] for k in (0, 1, 2, 3)))
        above = interface(*(w[k][c] for k in (1, 2, 3, 4)))
        keep[0, c, :, :width] = above
        keep[1, c, :, :width] = limited(w[2][c], below, above)[1]


def radial_face(src, cell, width, keep):
    w = [row_of(src, cell + k, width) for k in (0, 1, 2, 3)]
    highs, lows = [], []
    for c in range(5):
        below = keep[0, c, :, :width]
        above = interface(*(w[k][c] for k in (0, 1, 2, 3)))
        low, high = limited(w[1][c], below, above)
        highs.append(keep[1, c, :, :width])
        lows.append(low)
        keep[0, c, :, :width] = above
        keep[1, c, :, :width] = high
    return hllc(highs, lows, 1)


def stage_begin(src, cell, width, keep):
    radial_start(src, cell - 1, width, keep)
    flux = radial_face(src, cell - 1, width, keep)
    for c in range(5):
        keep[2, c, :, :width] = flux[c]


def stage_row(src, cell, width, keep, courant):
    upper = radial_face(src, cell, width, keep)
    total = []
    for c in range(5):
        total.append(COURANT_RADIAL * (upper[c] - keep[2, c, :, :width]))
        keep[2, c, :, :width] = upper[c]
    w = row_of(src, cell, width)
    for c, d in enumerate(polar_difference(w)):
        total[c] += COURANT_POLAR * d
    for c, d in enumerate(azimuth_difference(row_of(src, cell, src.shape[3]))):
        total[c] += courant * d[:, :width]
    return total


def stage_kernel(
    n_rad, block_ref, low_ref, up_ref, edge_ref, out_ref, wide_ref, first_ref, half_ref, keep1, keep2
):
    comps, rows, polar, cells = block_ref.shape
    rad = lax.axis_index("rad")
    total_rows = rows * n_rad
    lane = lax.broadcasted_iota(jnp.int32, (polar, LANES), 1)

    is_first, is_last = rad == 0, rad == n_rad - 1
    for c in range(comps):
        for r in range(rows):
            wide_ref[c, DEEP + r, :, :cells] = block_ref[c, r]
        for r in range(DEEP):
            wide_ref[c, r, :, :cells] = jnp.where(is_first, block_ref[c, 0], low_ref[c, rows - DEEP + r])
            wide_ref[c, DEEP + rows + r, :, :cells] = jnp.where(
                is_last, block_ref[c, rows - 1], up_ref[c, r]
            )

    def unpacked(which, c, r):
        plane = c * rows + r
        tile, slot = plane // PER_TILE, plane % PER_TILE
        after = rolled(edge_ref[which, tile], -slot * SLOT, 1)
        before = rolled(edge_ref[3 + which, tile], -(slot * SLOT + SLOT), 1)
        return jnp.where(lane < SLOT, after, before)

    for c in range(comps):
        own = [unpacked(1, c, r) for r in range(rows)]
        for r in range(rows):
            wide_ref[c, DEEP + r, :, cells:] = own[r]
        for r in range(DEEP):
            wide_ref[c, r, :, cells:] = jnp.where(is_first, own[0], unpacked(0, c, rows - DEEP + r))
            wide_ref[c, DEEP + rows + r, :, cells:] = jnp.where(is_last, own[rows - 1], unpacked(2, c, r))

    def courant_of(row):
        index = jnp.full((1, 1), rad * rows + row, jnp.int32).astype(jnp.float32)
        return COURANT_AZIMUTH / (1.0 + (index + 0.5) / total_rows)

    width = cells + LANES
    stage_begin(wide_ref, 3, width, keep1)

    def first_row(k, carry):
        change = stage_row(wide_ref, k + 3, width, keep1, courant_of(k - 3))
        start = conserved_of(row_of(wide_ref, k + 3, width))
        new = [a - b for a, b in zip(start, change)]
        w = primitive_of(new)
        for c in range(comps):
            first_ref[c, k, :, :] = w[c]
            half_ref[c, k, :, :] = (0.5 * start[c] + 0.5 * new[c])[:, :cells]
        return carry

    lax.fori_loop(0, rows + 6, first_row, 0)

    @pl.when(is_first)
    def _():
        for r in range(3):
            first_ref[:, r] = first_ref[:, 3]

    @pl.when(is_last)
    def _():
        for r in range(3):
            first_ref[:, rows + 3 + r] = first_ref[:, rows + 2]

    stage_begin(first_ref, 3, cells, keep2)

    def second_row(i, carry):
        change = stage_row(first_ref, i + 3, cells, keep2, courant_of(i))
        w = primitive_of([half_ref[c, i + 3] - 0.5 * change[c] for c in range(comps)])
        for c in range(comps):
            out_ref[i, c] = w[c]
        return carry

    lax.fori_loop(0, rows, second_row, 0)


def turn_kernel(n_az, planes_ref, shifts_ref, out_ref, far_ref, send_sem, recv_sem):
    rad, az = lax.axis_index("rad"), lax.axis_index("az")
    rows, comps, polar, cells = planes_ref.shape
    barrier = pltpu.get_barrier_semaphore()
    for d in range(1, REACH + 1):
        for column in (lax.rem(az + d, n_az), lax.rem(az + n_az - d, n_az)):
            pl.semaphore_signal(
                barrier, inc=1, device_id={"rad": rad, "az": column}, device_id_type=MESH
            )
    pl.semaphore_wait(barrier, 2 * REACH)

    def send(d):
        return pltpu.make_async_remote_copy(
            src_ref=planes_ref,
            dst_ref=far_ref.at[d - 1],
            send_sem=send_sem.at[d - 1],
            recv_sem=recv_sem.at[d - 1],
            device_id={"rad": rad, "az": lax.rem(az + d, n_az)},
            device_id_type=MESH,
        )

    for d in range(1, REACH + 1):
        send(d).start()
    for d in range(1, REACH + 1):
        send(d).wait()
    lane = lax.broadcasted_iota(jnp.int32, (polar, cells), 1)
    for i in range(rows):
        amount = shifts_ref[i]
        quotient = amount // cells
        rest = amount - quotient * cells
        for c in range(comps):
            blocks = [planes_ref[i, c]] + [far_ref[d, i, c] for d in range(REACH)]
            near, far = blocks[0], blocks[1]
            for d in range(1, REACH + 1):
                near = jnp.where(quotient == d, blocks[d], near)
                if d < REACH:
                    far = jnp.where(quotient == d, blocks[d + 1], far)
            out_ref[c, i] = pltpu.roll(jnp.where(lane >= cells - rest, far, near), rest, 1)


def on_device(n_rad, n_az, fields, shifts):
    comps, rows, polar, cells = fields.shape
    vmem = pl.BlockSpec(memory_space=pltpu.VMEM)
    tiles = -(-comps * rows // PER_TILE)
    f32 = functools.partial(jax.ShapeDtypeStruct, dtype=jnp.float32)
    low, up, edges = pl.pallas_call(
        functools.partial(halo_kernel, n_rad, n_az),
        out_shape=(f32(fields.shape), f32(fields.shape), f32((6, tiles, polar, LANES))),
        in_specs=[vmem],
        out_specs=(vmem, vmem, vmem),
        scratch_shapes=[
            pltpu.VMEM((2, tiles, polar, LANES), jnp.float32),
            pltpu.SemaphoreType.DMA((8,)),
            pltpu.SemaphoreType.DMA((8,)),
        ],
        compiler_params=pltpu.CompilerParams(collective_id=0, has_side_effects=True),
        name="halo",
    )(fields)
    width = cells + LANES
    planes = pl.pallas_call(
        functools.partial(stage_kernel, n_rad),
        out_shape=f32((rows, comps, polar, cells)),
        in_specs=[vmem] * 4,
        out_specs=vmem,
        scratch_shapes=[
            pltpu.VMEM((comps, rows + 2 * DEEP, polar, width), jnp.float32),
            pltpu.VMEM((comps, rows + DEEP, polar, width), jnp.float32),
            pltpu.VMEM((comps, rows + DEEP, polar, cells), jnp.float32),
            pltpu.VMEM((3, comps, polar, width), jnp.float32),
            pltpu.VMEM((3, comps, polar, width), jnp.float32),
        ],
        compiler_params=pltpu.CompilerParams(vmem_limit_bytes=32 * 1024 * 1024),
        name="stages",
    )(fields, low, up, edges)
    return pl.pallas_call(
        functools.partial(turn_kernel, n_az),
        out_shape=f32(fields.shape),
        in_specs=[vmem, pl.BlockSpec(memory_space=pltpu.SMEM)],
        out_specs=vmem,
        scratch_shapes=[
            pltpu.VMEM((REACH, rows, comps, polar, cells), jnp.float32),
            pltpu.SemaphoreType.DMA((REACH,)),
            pltpu.SemaphoreType.DMA((REACH,)),
        ],
        compiler_params=pltpu.CompilerParams(collective_id=1, has_side_effects=True),
        name="turn",
    )(planes, shifts)


def solution(mesh):
    return jax.shard_map(
        functools.partial(on_device, mesh.shape["rad"], mesh.shape["az"]),
        mesh=mesh,
        in_specs=(P(None, "rad", None, "az"), P("rad")),
        out_specs=P(None, "rad", None, "az"),
        check_vma=False,
    )
```

```python
import functools

import jax
import jax.numpy as jnp
from jax import lax
from jax.experimental import pallas as pl
from jax.experimental.pallas import tpu as pltpu
from jax.sharding import PartitionSpec as P

ADIABATIC = 1.4
COURANT_RADIAL = 0.09
COURANT_POLAR = 0.08
COURANT_AZIMUTH = 0.18
MESH = pl.DeviceIdType.MESH
LANES = 128
DEEP = 6
SLOT = 8
PER_TILE = LANES // SLOT
REACH = 3


def pack_edges(block_ref, pack_ref, side):
    comps, rows, polar, cells = block_ref.shape
    lane = lax.broadcasted_iota(jnp.int32, (polar, LANES), 1) // SLOT
    start = 0 if side == 0 else cells - LANES
    for tile in range(pack_ref.shape[1]):
        total = jnp.zeros((polar, LANES), jnp.float32)
        for slot in range(PER_TILE):
            plane = tile * PER_TILE + slot
            if plane < comps * rows:
                part = block_ref[plane // rows, plane % rows, :, start : start + LANES]
                amount = (slot * SLOT + (0 if side == 0 else SLOT)) % LANES
                if amount:
                    part = pltpu.roll(part, amount, 1)
                total = jnp.where(lane == slot, part, total)
        pack_ref[side, tile] = total


def halo_kernel(n_rad, n_az, block_ref, low_ref, up_ref, edge_ref, pack_ref, send_sem, recv_sem):
    rad, az = lax.axis_index("rad"), lax.axis_index("az")
    right, left = lax.rem(az + 1, n_az), lax.rem(az + n_az - 1, n_az)
    has = {-1: rad > 0, 1: rad < n_rad - 1}

    def when(step, work):
        if step == 0:
            work()
        else:
            pl.when(has[step])(work)

    barrier = pltpu.get_barrier_semaphore()

    def greet(step):
        def work():
            for column in (left, right) if step == 0 else (az, left, right):
                pl.semaphore_signal(
                    barrier, inc=1, device_id={"rad": rad + step, "az": column}, device_id_type=MESH
                )

        return work

    for step in (0, -1, 1):
        when(step, greet(step))
    inside = jnp.logical_and(has[-1], has[1])
    pl.semaphore_wait(barrier, jnp.where(inside, 8, 5 if n_rad > 1 else 2))

    def radial(step):
        return pltpu.make_async_remote_copy(
            src_ref=block_ref,
            dst_ref=up_ref if step < 0 else low_ref,
            send_sem=send_sem.at[0 if step < 0 else 1],
            recv_sem=recv_sem.at[0 if step < 0 else 1],
            device_id={"rad": rad + step, "az": az},
            device_id_type=MESH,
        )

    def edge(step, side):
        slot = side * 3 + 1 - step
        return pltpu.make_async_remote_copy(
            src_ref=pack_ref.at[side],
            dst_ref=edge_ref.at[slot],
            send_sem=send_sem.at[2 + slot],
            recv_sem=recv_sem.at[2 + slot],
            device_id={"rad": rad + step, "az": left if side == 0 else right},
            device_id_type=MESH,
        )

    for step in (-1, 1):
        when(step, lambda step=step: radial(step).start())
    for side in (0, 1):
        pack_edges(block_ref, pack_ref, side)
        for step in (0, -1, 1):
            when(step, lambda step=step, side=side: edge(step, side).start())
    for side in (0, 1):
        for step in (0, -1, 1):
            when(step, lambda step=step, side=side: edge(step, side).wait_send())
            when(-step, lambda step=step, side=side: edge(step, side).wait_recv())
    for step in (-1, 1):
        when(step, lambda step=step: radial(step).wait_send())
        when(-step, lambda step=step: radial(step).wait_recv())


def interface(before, centre, follow, beyond):
    value = 7.0 / 12.0 * (centre + follow) - 1.0 / 12.0 * (before + beyond)
    return jnp.clip(value, jnp.minimum(centre, follow), jnp.maximum(centre, follow))


def limited(u, left, right):
    flat = (right - u) * (u - left) <= 0.0
    spread = right - left
    middle = u - 0.5 * (left + right)
    product = spread * middle
    sixth = spread * spread * (1.0 / 6.0)
    triple = 3.0 * u
    new_left = jnp.where(flat, u, jnp.where(product > sixth, triple - 2.0 * right, left))
    new_right = jnp.where(flat, u, jnp.where(product < -sixth, triple - 2.0 * left, right))
    return new_left, new_right


def hllc(left, right, normal):
    gas_left, gas_right = ADIABATIC * left[4], ADIABATIC * right[4]
    sound_left = gas_left * lax.rsqrt(gas_left * left[0])
    sound_right = gas_right * lax.rsqrt(gas_right * right[0])
    u_left, u_right = left[normal], right[normal]
    slow = jnp.minimum(u_left - sound_left, u_right - sound_right)
    fast = jnp.maximum(u_left + sound_left, u_right + sound_right)
    mass_left = left[0] * (u_left - slow)
    mass_right = right[0] * (fast - u_right)
    contact = (mass_left * u_left + mass_right * u_right + left[4] - right[4]) / (
        mass_left + mass_right
    )
    supersonic = slow >= 0.0
    from_left = jnp.logical_or(supersonic, contact >= 0.0)
    rho, v1, v2, v3, p = [jnp.where(from_left, a, b) for a, b in zip(left, right)]
    speeds = (None, v1, v2, v3)
    u = speeds[normal]
    wave = jnp.where(from_left, slow, fast)
    star = jnp.logical_and(slow < 0.0, jnp.logical_or(from_left, fast > 0.0))
    energy = p * (1.0 / (ADIABATIC - 1.0)) + 0.5 * rho * (v1 * v1 + v2 * v2 + v3 * v3)
    momentum = rho * u
    relative = wave - u
    mass = rho * relative
    inverse = 1.0 / (wave - contact)
    factor = mass * inverse
    star_energy = inverse * (relative * energy + (contact - u) * (mass * contact + p))
    flux_mass = momentum + jnp.where(star, wave * (factor - rho), 0.0)
    flux_normal = momentum * u + p + jnp.where(star, wave * (factor * contact - momentum), 0.0)
    flux_energy = (energy + p) * u + jnp.where(star, wave * (star_energy - energy), 0.0)
    out = [flux_mass, None, None, None, flux_energy]
    for axis in (1, 2, 3):
        out[axis] = flux_normal if axis == normal else speeds[axis] * flux_mass
    return out


def conserved_of(w):
    energy = w[4] * (1.0 / (ADIABATIC - 1.0)) + 0.5 * w[0] * (
        w[1] * w[1] + w[2] * w[2] + w[3] * w[3]
    )
    return [w[0], w[0] * w[1], w[0] * w[2], w[0] * w[3], energy]


def primitive_of(u):
    inverse = 1.0 / u[0]
    v = [inverse * u[k] for k in (1, 2, 3)]
    squared = v[0] * v[0] + v[1] * v[1] + v[2] * v[2]
    return [u[0]] + v + [(ADIABATIC - 1.0) * (u[4] - 0.5 * u[0] * squared)]


def rolled(x, amount, axis):
    return pltpu.roll(x, amount % x.shape[axis], axis)


def azimuth_difference(w):
    lows, highs = [], []
    for u in w:
        edge = interface(rolled(u, 1, 1), u, rolled(u, -1, 1), rolled(u, -2, 1))
        low, high = limited(u, rolled(edge, 1, 1), edge)
        lows.append(low)
        highs.append(rolled(high, 1, 1))
    flux = hllc(highs, lows, 3)
    return [rolled(f, -1, 1) - f for f in flux]


def polar_difference(w):
    count = w[0].shape[0]
    place = lax.broadcasted_iota(jnp.int32, w[0].shape, 0)
    first, last = place == 0, place == count - 1
    beyond_last = place >= count - 2
    lows, highs = [], []
    for u in w:
        before = jnp.where(first, u, rolled(u, 1, 0))
        follow = jnp.where(last, u, rolled(u, -1, 0))
        beyond = jnp.where(beyond_last, jnp.where(last, u, follow), rolled(u, -2, 0))
        edge = interface(before, u, follow, beyond)
        low, high = limited(u, jnp.where(first, u, rolled(edge, 1, 0)), edge)
        lows.append(low)
        highs.append(jnp.where(first, u, rolled(high, 1, 0)))
    flux = hllc(highs, lows, 2)
    rho, v1, v2, v3, p = w
    momentum = rho * v2
    energy = conserved_of(w)[4]
    outer = [momentum, momentum * v1, momentum * v2 + p, momentum * v3, (energy + p) * v2]
    return [jnp.where(last, o, rolled(f, -1, 0)) - f for f, o in zip(flux, outer)]


def row_of(ref, row, width):
    return [ref[c, row, :, :width] for c in range(5)]


def radial_start(src, cell, width, keep):
    w = [row_of(src, cell + k, width) for k in (-2, -1, 0, 1, 2)]
    for c in range(5):
        below = interface(*(w[k][c] for k in (0, 1, 2, 3)))
        above = interface(*(w[k][c] for k in (1, 2, 3, 4)))
        keep[0, c, :, :width] = above
        keep[1, c, :, :width] = limited(w[2][c], below, above)[1]


def radial_face(src, cell, width, keep):
    w = [row_of(src, cell + k, width) for k in (0, 1, 2, 3)]
    highs, lows = [], []
    for c in range(5):
        below = keep[0, c, :, :width]
        above = interface(*(w[k][c] for k in (0, 1, 2, 3)))
        low, high = limited(w[1][c], below, above)
        highs.append(keep[1, c, :, :width])
        lows.append(low)
        keep[0, c, :, :width] = above
        keep[1, c, :, :width] = high
    return hllc(highs, lows, 1)


def stage_begin(src, cell, width, keep):
    radial_start(src, cell - 1, width, keep)
    flux = radial_face(src, cell - 1, width, keep)
    for c in range(5):
        keep[2, c, :, :width] = flux[c]


def stage_row(src, cell, width, keep, courant):
    upper = radial_face(src, cell, width, keep)
    total = []
    for c in range(5):
        total.append(COURANT_RADIAL * (upper[c] - keep[2, c, :, :width]))
        keep[2, c, :, :width] = upper[c]
    w = row_of(src, cell, width)
    for c, d in enumerate(polar_difference(w)):
        total[c] += COURANT_POLAR * d
    for c, d in enumerate(azimuth_difference(row_of(src, cell, src.shape[3]))):
        total[c] += courant * d[:, :width]
    return total


def stage_kernel(
    n_rad, block_ref, low_ref, up_ref, edge_ref, out_ref, wide_ref, first_ref, half_ref, keep1, keep2
):
    comps, rows, polar, cells = block_ref.shape
    rad = lax.axis_index("rad")
    total_rows = rows * n_rad
    lane = lax.broadcasted_iota(jnp.int32, (polar, LANES), 1)

    is_first, is_last = rad == 0, rad == n_rad - 1
    for c in range(comps):
        for r in range(rows):
            wide_ref[c, DEEP + r, :, :cells] = block_ref[c, r]
        for r in range(DEEP):
            wide_ref[c, r, :, :cells] = jnp.where(is_first, block_ref[c, 0], low_ref[c, rows - DEEP + r])
            wide_ref[c, DEEP + rows + r, :, :cells] = jnp.where(
                is_last, block_ref[c, rows - 1], up_ref[c, r]
            )

    def unpacked(which, c, r):
        plane = c * rows + r
        tile, slot = plane // PER_TILE, plane % PER_TILE
        after = rolled(edge_ref[which, tile], -slot * SLOT, 1)
        before = rolled(edge_ref[3 + which, tile], -(slot * SLOT + SLOT), 1)
        return jnp.where(lane < SLOT, after, before)

    for c in range(comps):
        own = [unpacked(1, c, r) for r in range(rows)]
        for r in range(rows):
            wide_ref[c, DEEP + r, :, cells:] = own[r]
        for r in range(DEEP):
            wide_ref[c, r, :, cells:] = jnp.where(is_first, own[0], unpacked(0, c, rows - DEEP + r))
            wide_ref[c, DEEP + rows + r, :, cells:] = jnp.where(is_last, own[rows - 1], unpacked(2, c, r))

    def courant_of(row):
        index = jnp.full((1, 1), rad * rows + row, jnp.int32).astype(jnp.float32)
        return COURANT_AZIMUTH / (1.0 + (index + 0.5) / total_rows)

    width = cells + LANES
    stage_begin(wide_ref, 3, width, keep1)

    def first_row(k, carry):
        change = stage_row(wide_ref, k + 3, width, keep1, courant_of(k - 3))
        start = conserved_of(row_of(wide_ref, k + 3, width))
        new = [a - b for a, b in zip(start, change)]
        w = primitive_of(new)
        for c in range(comps):
            first_ref[c, k, :, :] = w[c]
            half_ref[c, k, :, :] = (0.5 * start[c] + 0.5 * new[c])[:, :cells]
        return carry

    lax.fori_loop(0, rows + 6, first_row, 0)

    @pl.when(is_first)
    def _():
        for r in range(3):
            first_ref[:, r] = first_ref[:, 3]

    @pl.when(is_last)
    def _():
        for r in range(3):
            first_ref[:, rows + 3 + r] = first_ref[:, rows + 2]

    for spare in range(rows * comps, out_ref.shape[0]):
        out_ref[spare] = jnp.zeros((polar, cells), jnp.float32)
    stage_begin(first_ref, 3, cells, keep2)

    def second_row(i, carry):
        change = stage_row(first_ref, i + 3, cells, keep2, courant_of(i))
        w = primitive_of([half_ref[c, i + 3] - 0.5 * change[c] for c in range(comps)])
        for c in range(comps):
            out_ref[i * comps + c] = w[c]
        return carry

    lax.fori_loop(0, rows, second_row, 0)


def turn_kernel(n_az, planes_ref, shifts_ref, out_ref, far_ref, send_sem, recv_sem):
    rad, az = lax.axis_index("rad"), lax.axis_index("az")
    comps, rows, polar, cells = out_ref.shape
    barrier = pltpu.get_barrier_semaphore()
    for d in range(1, REACH + 1):
        for column in (lax.rem(az + d, n_az), lax.rem(az + n_az - d, n_az)):
            pl.semaphore_signal(
                barrier, inc=1, device_id={"rad": rad, "az": column}, device_id_type=MESH
            )
    pl.semaphore_wait(barrier, 2 * REACH)

    def send(d):
        return pltpu.make_async_remote_copy(
            src_ref=planes_ref,
            dst_ref=far_ref.at[d - 1],
            send_sem=send_sem.at[d - 1],
            recv_sem=recv_sem.at[d - 1],
            device_id={"rad": rad, "az": lax.rem(az + d, n_az)},
            device_id_type=MESH,
        )

    for d in range(1, REACH + 1):
        send(d).start()
    for d in range(1, REACH + 1):
        send(d).wait()
    lane = lax.broadcasted_iota(jnp.int32, (polar, cells), 1)
    for i in range(rows):
        amount = shifts_ref[i]
        quotient = amount // cells
        rest = amount - quotient * cells
        for c in range(comps):
            blocks = [planes_ref[i * comps + c]] + [far_ref[d, i * comps + c] for d in range(REACH)]
            near, far = blocks[0], blocks[1]
            for d in range(1, REACH + 1):
                near = jnp.where(quotient == d, blocks[d], near)
                if d < REACH:
                    far = jnp.where(quotient == d, blocks[d + 1], far)
            out_ref[c, i] = pltpu.roll(jnp.where(lane >= cells - rest, far, near), rest, 1)


def quarter_turn_kernel(n_az, planes_ref, shifts_ref, out_ref, far_ref, turned_ref, back_ref, send_sem, recv_sem):
    rad, az = lax.axis_index("rad"), lax.axis_index("az")
    comps, rows, polar, cells = out_ref.shape
    share = planes_ref.shape[0] // n_az
    barrier = pltpu.get_barrier_semaphore()
    for d in range(1, n_az):
        pl.semaphore_signal(
            barrier, inc=1, device_id={"rad": rad, "az": lax.rem(az + d, n_az)}, device_id_type=MESH
        )
    pl.semaphore_wait(barrier, n_az - 1)

    def gather(d):
        owner = lax.rem(az + d, n_az)
        return pltpu.make_async_remote_copy(
            src_ref=planes_ref.at[pl.ds(owner * share, share)],
            dst_ref=far_ref.at[d - 1],
            send_sem=send_sem.at[d - 1],
            recv_sem=recv_sem.at[d - 1],
            device_id={"rad": rad, "az": owner},
            device_id_type=MESH,
        )

    def home(g):
        return pltpu.make_async_remote_copy(
            src_ref=turned_ref.at[g],
            dst_ref=back_ref.at[pl.ds(az * share, share)],
            send_sem=send_sem.at[n_az - 2 + g],
            recv_sem=recv_sem.at[n_az - 2 + g],
            device_id={"rad": rad, "az": lax.rem(az + g, n_az)},
            device_id_type=MESH,
        )

    for d in range(1, n_az):
        gather(d).start()
    for d in range(1, n_az):
        gather(d).wait()
    lane = lax.broadcasted_iota(jnp.int32, (polar, cells), 1)
    for k in range(share):
        row = jnp.minimum((az * share + k) // comps, rows - 1)
        amount = shifts_ref[row]
        quotient = amount // cells
        rest = amount - quotient * cells
        blocks = [planes_ref[az * share + k]] + [far_ref[d, k] for d in range(n_az - 1)]
        blocks = [pltpu.roll(b, rest, 1) for b in blocks]
        ahead = blocks
        for q in range(1, n_az):
            ahead = [
                jnp.where(quotient == q, blocks[(q + j) % n_az], a) for j, a in enumerate(ahead)
            ]
        for g in range(n_az):
            turned = jnp.where(lane < rest, ahead[(1 - g) % n_az], ahead[-g % n_az])
            if g:
                turned_ref[g, k] = turned
            else:
                back_ref[az * share + k] = turned
    for g in range(1, n_az):
        home(g).start()
    for g in range(1, n_az):
        home(g).wait_send()
        sender = lax.rem(az + n_az - g, n_az)
        pltpu.make_async_remote_copy(
            src_ref=turned_ref.at[g],
            dst_ref=back_ref.at[pl.ds(sender * share, share)],
            send_sem=send_sem.at[n_az - 2 + g],
            recv_sem=recv_sem.at[n_az - 2 + g],
            device_id={"rad": rad, "az": lax.rem(az + g, n_az)},
            device_id_type=MESH,
        ).wait_recv()
    for i in range(rows):
        for c in range(comps):
            out_ref[c, i] = back_ref[i * comps + c]


def on_device(n_rad, n_az, fields, shifts):
    comps, rows, polar, cells = fields.shape
    vmem = pl.BlockSpec(memory_space=pltpu.VMEM)
    tiles = -(-comps * rows // PER_TILE)
    f32 = functools.partial(jax.ShapeDtypeStruct, dtype=jnp.float32)
    low, up, edges = pl.pallas_call(
        functools.partial(halo_kernel, n_rad, n_az),
        out_shape=(f32(fields.shape), f32(fields.shape), f32((6, tiles, polar, LANES))),
        in_specs=[vmem],
        out_specs=(vmem, vmem, vmem),
        scratch_shapes=[
            pltpu.VMEM((2, tiles, polar, LANES), jnp.float32),
            pltpu.SemaphoreType.DMA((8,)),
            pltpu.SemaphoreType.DMA((8,)),
        ],
        compiler_params=pltpu.CompilerParams(collective_id=0, has_side_effects=True),
        name="halo",
    )(fields)
    width = cells + LANES
    count = -(-rows * comps // 8) * 8
    planes = pl.pallas_call(
        functools.partial(stage_kernel, n_rad),
        out_shape=f32((count, polar, cells)),
        in_specs=[vmem] * 4,
        out_specs=vmem,
        scratch_shapes=[
            pltpu.VMEM((comps, rows + 2 * DEEP, polar, width), jnp.float32),
            pltpu.VMEM((comps, rows + DEEP, polar, width), jnp.float32),
            pltpu.VMEM((comps, rows + DEEP, polar, cells), jnp.float32),
            pltpu.VMEM((3, comps, polar, width), jnp.float32),
            pltpu.VMEM((3, comps, polar, width), jnp.float32),
        ],
        compiler_params=pltpu.CompilerParams(vmem_limit_bytes=32 * 1024 * 1024),
        name="stages",
    )(fields, low, up, edges)
    if n_az == 4:
        share = count // n_az
        return pl.pallas_call(
            functools.partial(quarter_turn_kernel, n_az),
            out_shape=f32(fields.shape),
            in_specs=[vmem, pl.BlockSpec(memory_space=pltpu.SMEM)],
            out_specs=vmem,
            scratch_shapes=[
                pltpu.VMEM((n_az - 1, share, polar, cells), jnp.float32),
                pltpu.VMEM((n_az, share, polar, cells), jnp.float32),
                pltpu.VMEM((count, polar, cells), jnp.float32),
                pltpu.SemaphoreType.DMA((2 * n_az - 2,)),
                pltpu.SemaphoreType.DMA((2 * n_az - 2,)),
            ],
            compiler_params=pltpu.CompilerParams(collective_id=1, has_side_effects=True),
            name="turn",
        )(planes, shifts)
    return pl.pallas_call(
        functools.partial(turn_kernel, n_az),
        out_shape=f32(fields.shape),
        in_specs=[vmem, pl.BlockSpec(memory_space=pltpu.SMEM)],
        out_specs=vmem,
        scratch_shapes=[
            pltpu.VMEM((REACH, count, polar, cells), jnp.float32),
            pltpu.SemaphoreType.DMA((REACH,)),
            pltpu.SemaphoreType.DMA((REACH,)),
        ],
        compiler_params=pltpu.CompilerParams(collective_id=1, has_side_effects=True),
        name="turn",
    )(planes, shifts)


def solution(mesh):
    return jax.shard_map(
        functools.partial(on_device, mesh.shape["rad"], mesh.shape["az"]),
        mesh=mesh,
        in_specs=(P(None, "rad", None, "az"), P("rad")),
        out_specs=P(None, "rad", None, "az"),
        check_vma=False,
    )
```

```python
import functools

import jax
import jax.numpy as jnp
from jax import lax
from jax.experimental import pallas as pl
from jax.experimental.pallas import tpu as pltpu
from jax.sharding import PartitionSpec as P

ADIABATIC = 1.4
COURANT_RADIAL = 0.09
COURANT_POLAR = 0.08
COURANT_AZIMUTH = 0.18
MESH = pl.DeviceIdType.MESH
LANES = 128
DEEP = 6
SLOT = 8
PER_TILE = LANES // SLOT
REACH = 3


def pack_edges(block_ref, pack_ref, side):
    comps, rows, polar, cells = block_ref.shape
    lane = lax.broadcasted_iota(jnp.int32, (polar, LANES), 1) // SLOT
    start = 0 if side == 0 else cells - LANES
    for tile in range(pack_ref.shape[1]):
        total = jnp.zeros((polar, LANES), jnp.float32)
        for slot in range(PER_TILE):
            plane = tile * PER_TILE + slot
            if plane < comps * rows:
                part = block_ref[plane // rows, plane % rows, :, start : start + LANES]
                amount = (slot * SLOT + (0 if side == 0 else SLOT)) % LANES
                if amount:
                    part = pltpu.roll(part, amount, 1)
                total = jnp.where(lane == slot, part, total)
        pack_ref[side, tile] = total


def halo_kernel(n_rad, n_az, block_ref, low_ref, up_ref, edge_ref, pack_ref, send_sem, recv_sem):
    rad, az = lax.axis_index("rad"), lax.axis_index("az")
    right, left = lax.rem(az + 1, n_az), lax.rem(az + n_az - 1, n_az)
    has = {-1: rad > 0, 1: rad < n_rad - 1}

    def when(step, work):
        if step == 0:
            work()
        else:
            pl.when(has[step])(work)

    barrier = pltpu.get_barrier_semaphore()

    def greet(step):
        def work():
            for column in (left, right) if step == 0 else (az, left, right):
                pl.semaphore_signal(
                    barrier, inc=1, device_id={"rad": rad + step, "az": column}, device_id_type=MESH
                )

        return work

    for step in (0, -1, 1):
        when(step, greet(step))
    inside = jnp.logical_and(has[-1], has[1])
    pl.semaphore_wait(barrier, jnp.where(inside, 8, 5 if n_rad > 1 else 2))

    def radial(step):
        return pltpu.make_async_remote_copy(
            src_ref=block_ref,
            dst_ref=up_ref if step < 0 else low_ref,
            send_sem=send_sem.at[0 if step < 0 else 1],
            recv_sem=recv_sem.at[0 if step < 0 else 1],
            device_id={"rad": rad + step, "az": az},
            device_id_type=MESH,
        )

    def edge(step, side):
        slot = side * 3 + 1 - step
        return pltpu.make_async_remote_copy(
            src_ref=pack_ref.at[side],
            dst_ref=edge_ref.at[slot],
            send_sem=send_sem.at[2 + slot],
            recv_sem=recv_sem.at[2 + slot],
            device_id={"rad": rad + step, "az": left if side == 0 else right},
            device_id_type=MESH,
        )

    for step in (-1, 1):
        when(step, lambda step=step: radial(step).start())
    for side in (0, 1):
        pack_edges(block_ref, pack_ref, side)
        for step in (0, -1, 1):
            when(step, lambda step=step, side=side: edge(step, side).start())
    for side in (0, 1):
        for step in (0, -1, 1):
            when(step, lambda step=step, side=side: edge(step, side).wait_send())
            when(-step, lambda step=step, side=side: edge(step, side).wait_recv())
    for step in (-1, 1):
        when(step, lambda step=step: radial(step).wait_send())
        when(-step, lambda step=step: radial(step).wait_recv())


def interface(before, centre, follow, beyond):
    value = 7.0 / 12.0 * (centre + follow) - 1.0 / 12.0 * (before + beyond)
    return jnp.clip(value, jnp.minimum(centre, follow), jnp.maximum(centre, follow))


def limited(u, left, right):
    flat = (right - u) * (u - left) <= 0.0
    spread = right - left
    middle = u - 0.5 * (left + right)
    product = spread * middle
    sixth = spread * spread * (1.0 / 6.0)
    triple = 3.0 * u
    new_left = jnp.where(flat, u, jnp.where(product > sixth, triple - 2.0 * right, left))
    new_right = jnp.where(flat, u, jnp.where(product < -sixth, triple - 2.0 * left, right))
    return new_left, new_right


def hllc(left, right, normal):
    gas_left, gas_right = ADIABATIC * left[4], ADIABATIC * right[4]
    sound_left = gas_left * lax.rsqrt(gas_left * left[0])
    sound_right = gas_right * lax.rsqrt(gas_right * right[0])
    u_left, u_right = left[normal], right[normal]
    slow = jnp.minimum(u_left - sound_left, u_right - sound_right)
    fast = jnp.maximum(u_left + sound_left, u_right + sound_right)
    mass_left = left[0] * (u_left - slow)
    mass_right = right[0] * (fast - u_right)
    contact = (mass_left * u_left + mass_right * u_right + left[4] - right[4]) / (
        mass_left + mass_right
    )
    supersonic = slow >= 0.0
    from_left = jnp.logical_or(supersonic, contact >= 0.0)
    rho, v1, v2, v3, p = [jnp.where(from_left, a, b) for a, b in zip(left, right)]
    speeds = (None, v1, v2, v3)
    u = speeds[normal]
    wave = jnp.where(from_left, slow, fast)
    star = jnp.logical_and(slow < 0.0, jnp.logical_or(from_left, fast > 0.0))
    energy = p * (1.0 / (ADIABATIC - 1.0)) + 0.5 * rho * (v1 * v1 + v2 * v2 + v3 * v3)
    momentum = rho * u
    relative = wave - u
    mass = rho * relative
    inverse = 1.0 / (wave - contact)
    factor = mass * inverse
    star_energy = inverse * (relative * energy + (contact - u) * (mass * contact + p))
    flux_mass = momentum + jnp.where(star, wave * (factor - rho), 0.0)
    flux_normal = momentum * u + p + jnp.where(star, wave * (factor * contact - momentum), 0.0)
    flux_energy = (energy + p) * u + jnp.where(star, wave * (star_energy - energy), 0.0)
    out = [flux_mass, None, None, None, flux_energy]
    for axis in (1, 2, 3):
        out[axis] = flux_normal if axis == normal else speeds[axis] * flux_mass
    return out


def conserved_of(w):
    energy = w[4] * (1.0 / (ADIABATIC - 1.0)) + 0.5 * w[0] * (
        w[1] * w[1] + w[2] * w[2] + w[3] * w[3]
    )
    return [w[0], w[0] * w[1], w[0] * w[2], w[0] * w[3], energy]


def primitive_of(u):
    inverse = 1.0 / u[0]
    v = [inverse * u[k] for k in (1, 2, 3)]
    squared = v[0] * v[0] + v[1] * v[1] + v[2] * v[2]
    return [u[0]] + v + [(ADIABATIC - 1.0) * (u[4] - 0.5 * u[0] * squared)]


def rolled(x, amount, axis):
    return pltpu.roll(x, amount % x.shape[axis], axis)


def azimuth_difference(w):
    lows, highs = [], []
    for u in w:
        edge = interface(rolled(u, 1, 1), u, rolled(u, -1, 1), rolled(u, -2, 1))
        low, high = limited(u, rolled(edge, 1, 1), edge)
        lows.append(low)
        highs.append(rolled(high, 1, 1))
    flux = hllc(highs, lows, 3)
    return [rolled(f, -1, 1) - f for f in flux]


def polar_difference(w):
    count = w[0].shape[0]
    place = lax.broadcasted_iota(jnp.int32, w[0].shape, 0)
    first, last = place == 0, place == count - 1
    beyond_last = place >= count - 2
    lows, highs = [], []
    for u in w:
        before = jnp.where(first, u, rolled(u, 1, 0))
        follow = jnp.where(last, u, rolled(u, -1, 0))
        beyond = jnp.where(beyond_last, jnp.where(last, u, follow), rolled(u, -2, 0))
        edge = interface(before, u, follow, beyond)
        low, high = limited(u, jnp.where(first, u, rolled(edge, 1, 0)), edge)
        lows.append(low)
        highs.append(jnp.where(first, u, rolled(high, 1, 0)))
    flux = hllc(highs, lows, 2)
    rho, v1, v2, v3, p = w
    momentum = rho * v2
    energy = conserved_of(w)[4]
    outer = [momentum, momentum * v1, momentum * v2 + p, momentum * v3, (energy + p) * v2]
    return [jnp.where(last, o, rolled(f, -1, 0)) - f for f, o in zip(flux, outer)]


def row_of(ref, row, width):
    return [ref[c, row, :, :width] for c in range(5)]


def radial_start(src, cell, width, keep):
    w = [row_of(src, cell + k, width) for k in (-2, -1, 0, 1, 2)]
    for c in range(5):
        below = interface(*(w[k][c] for k in (0, 1, 2, 3)))
        above = interface(*(w[k][c] for k in (1, 2, 3, 4)))
        keep[0, c, :, :width] = above
        keep[1, c, :, :width] = limited(w[2][c], below, above)[1]


def radial_face(src, cell, width, keep):
    w = [row_of(src, cell + k, width) for k in (0, 1, 2, 3)]
    highs, lows = [], []
    for c in range(5):
        below = keep[0, c, :, :width]
        above = interface(*(w[k][c] for k in (0, 1, 2, 3)))
        low, high = limited(w[1][c], below, above)
        highs.append(keep[1, c, :, :width])
        lows.append(low)
        keep[0, c, :, :width] = above
        keep[1, c, :, :width] = high
    return hllc(highs, lows, 1)


def stage_begin(src, cell, width, keep):
    radial_start(src, cell - 1, width, keep)
    flux = radial_face(src, cell - 1, width, keep)
    for c in range(5):
        keep[2, c, :, :width] = flux[c]


def stage_row(src, cell, width, keep, courant):
    upper = radial_face(src, cell, width, keep)
    total = []
    for c in range(5):
        total.append(COURANT_RADIAL * (upper[c] - keep[2, c, :, :width]))
        keep[2, c, :, :width] = upper[c]
    w = row_of(src, cell, width)
    for c, d in enumerate(polar_difference(w)):
        total[c] += COURANT_POLAR * d
    for c, d in enumerate(azimuth_difference(row_of(src, cell, src.shape[3]))):
        total[c] += courant * d[:, :width]
    return total


def stage_kernel(
    n_rad, block_ref, low_ref, up_ref, edge_ref, out_ref, wide_ref, first_ref, half_ref, keep1, keep2
):
    comps, rows, polar, cells = block_ref.shape
    rad = lax.axis_index("rad")
    total_rows = rows * n_rad
    lane = lax.broadcasted_iota(jnp.int32, (polar, LANES), 1)

    is_first, is_last = rad == 0, rad == n_rad - 1
    for c in range(comps):
        for r in range(rows):
            wide_ref[c, DEEP + r, :, :cells] = block_ref[c, r]
        for r in range(DEEP):
            wide_ref[c, r, :, :cells] = jnp.where(is_first, block_ref[c, 0], low_ref[c, rows - DEEP + r])
            wide_ref[c, DEEP + rows + r, :, :cells] = jnp.where(
                is_last, block_ref[c, rows - 1], up_ref[c, r]
            )

    def unpacked(which, c, r):
        plane = c * rows + r
        tile, slot = plane // PER_TILE, plane % PER_TILE
        after = rolled(edge_ref[which, tile], -slot * SLOT, 1)
        before = rolled(edge_ref[3 + which, tile], -(slot * SLOT + SLOT), 1)
        return jnp.where(lane < SLOT, after, before)

    for c in range(comps):
        own = [unpacked(1, c, r) for r in range(rows)]
        for r in range(rows):
            wide_ref[c, DEEP + r, :, cells:] = own[r]
        for r in range(DEEP):
            wide_ref[c, r, :, cells:] = jnp.where(is_first, own[0], unpacked(0, c, rows - DEEP + r))
            wide_ref[c, DEEP + rows + r, :, cells:] = jnp.where(is_last, own[rows - 1], unpacked(2, c, r))

    def courant_of(row):
        index = jnp.full((1, 1), rad * rows + row, jnp.int32).astype(jnp.float32)
        return COURANT_AZIMUTH / (1.0 + (index + 0.5) / total_rows)

    width = cells + LANES
    stage_begin(wide_ref, 3, width, keep1)

    def first_row(k, carry):
        change = stage_row(wide_ref, k + 3, width, keep1, courant_of(k - 3))
        start = conserved_of(row_of(wide_ref, k + 3, width))
        new = [a - b for a, b in zip(start, change)]
        w = primitive_of(new)
        for c in range(comps):
            first_ref[c, k, :, :] = w[c]
            half_ref[c, k, :, :] = (0.5 * start[c] + 0.5 * new[c])[:, :cells]
        return carry

    lax.fori_loop(0, rows + 6, first_row, 0)

    @pl.when(is_first)
    def _():
        for r in range(3):
            first_ref[:, r] = first_ref[:, 3]

    @pl.when(is_last)
    def _():
        for r in range(3):
            first_ref[:, rows + 3 + r] = first_ref[:, rows + 2]

    for spare in range(rows * comps, out_ref.shape[0]):
        out_ref[spare] = jnp.zeros((polar, cells), jnp.float32)
    stage_begin(first_ref, 3, cells, keep2)

    def second_row(i, carry):
        change = stage_row(first_ref, i + 3, cells, keep2, courant_of(i))
        w = primitive_of([half_ref[c, i + 3] - 0.5 * change[c] for c in range(comps)])
        for c in range(comps):
            out_ref[i * comps + c] = w[c]
        return carry

    lax.fori_loop(0, rows, second_row, 0)


def turn_kernel(n_az, planes_ref, shifts_ref, out_ref, far_ref, send_sem, recv_sem):
    rad, az = lax.axis_index("rad"), lax.axis_index("az")
    comps, rows, polar, cells = out_ref.shape
    barrier = pltpu.get_barrier_semaphore()
    for d in range(1, REACH + 1):
        for column in (lax.rem(az + d, n_az), lax.rem(az + n_az - d, n_az)):
            pl.semaphore_signal(
                barrier, inc=1, device_id={"rad": rad, "az": column}, device_id_type=MESH
            )
    pl.semaphore_wait(barrier, 2 * REACH)

    def send(d):
        return pltpu.make_async_remote_copy(
            src_ref=planes_ref,
            dst_ref=far_ref.at[d - 1],
            send_sem=send_sem.at[d - 1],
            recv_sem=recv_sem.at[d - 1],
            device_id={"rad": rad, "az": lax.rem(az + d, n_az)},
            device_id_type=MESH,
        )

    for d in range(1, REACH + 1):
        send(d).start()
    for d in range(1, REACH + 1):
        send(d).wait()
    lane = lax.broadcasted_iota(jnp.int32, (polar, cells), 1)
    for i in range(rows):
        amount = shifts_ref[i]
        quotient = amount // cells
        rest = amount - quotient * cells
        for c in range(comps):
            blocks = [planes_ref[i * comps + c]] + [far_ref[d, i * comps + c] for d in range(REACH)]
            near, far = blocks[0], blocks[1]
            for d in range(1, REACH + 1):
                near = jnp.where(quotient == d, blocks[d], near)
                if d < REACH:
                    far = jnp.where(quotient == d, blocks[d + 1], far)
            out_ref[c, i] = pltpu.roll(jnp.where(lane >= cells - rest, far, near), rest, 1)


def quarter_turn_kernel(n_rad, n_az, block_ref, low_ref, up_ref, edge_ref, shifts_ref, out_ref, far_ref, turned_ref, back_ref, send_sem, recv_sem, planes_ref, *stage_refs):
    rad, az = lax.axis_index("rad"), lax.axis_index("az")
    comps, rows, polar, cells = out_ref.shape
    share = planes_ref.shape[0] // n_az
    barrier = pltpu.get_barrier_semaphore()
    for d in range(1, n_az):
        pl.semaphore_signal(
            barrier, inc=1, device_id={"rad": rad, "az": lax.rem(az + d, n_az)}, device_id_type=MESH
        )
    stage_kernel(n_rad, block_ref, low_ref, up_ref, edge_ref, planes_ref, *stage_refs)
    pl.semaphore_wait(barrier, n_az - 1)

    def gather(d):
        owner = lax.rem(az + d, n_az)
        return pltpu.make_async_remote_copy(
            src_ref=planes_ref.at[pl.ds(owner * share, share)],
            dst_ref=far_ref.at[d - 1],
            send_sem=send_sem.at[d - 1],
            recv_sem=recv_sem.at[d - 1],
            device_id={"rad": rad, "az": owner},
            device_id_type=MESH,
        )

    def home(g):
        return pltpu.make_async_remote_copy(
            src_ref=turned_ref.at[g],
            dst_ref=back_ref.at[pl.ds(az * share, share)],
            send_sem=send_sem.at[n_az - 2 + g],
            recv_sem=recv_sem.at[n_az - 2 + g],
            device_id={"rad": rad, "az": lax.rem(az + g, n_az)},
            device_id_type=MESH,
        )

    for d in range(1, n_az):
        gather(d).start()
    for d in range(1, n_az):
        gather(d).wait()
    lane = lax.broadcasted_iota(jnp.int32, (polar, cells), 1)
    for k in range(share):
        row = jnp.minimum((az * share + k) // comps, rows - 1)
        amount = shifts_ref[row]
        quotient = amount // cells
        rest = amount - quotient * cells
        blocks = [planes_ref[az * share + k]] + [far_ref[d, k] for d in range(n_az - 1)]
        blocks = [pltpu.roll(b, rest, 1) for b in blocks]
        ahead = blocks
        for q in range(1, n_az):
            ahead = [
                jnp.where(quotient == q, blocks[(q + j) % n_az], a) for j, a in enumerate(ahead)
            ]
        for g in range(n_az):
            turned = jnp.where(lane < rest, ahead[(1 - g) % n_az], ahead[-g % n_az])
            if g:
                turned_ref[g, k] = turned
            else:
                back_ref[az * share + k] = turned
    for g in range(1, n_az):
        home(g).start()
    for g in range(1, n_az):
        home(g).wait_send()
        sender = lax.rem(az + n_az - g, n_az)
        pltpu.make_async_remote_copy(
            src_ref=turned_ref.at[g],
            dst_ref=back_ref.at[pl.ds(sender * share, share)],
            send_sem=send_sem.at[n_az - 2 + g],
            recv_sem=recv_sem.at[n_az - 2 + g],
            device_id={"rad": rad, "az": lax.rem(az + g, n_az)},
            device_id_type=MESH,
        ).wait_recv()
    for i in range(rows):
        for c in range(comps):
            out_ref[c, i] = back_ref[i * comps + c]


def on_device(n_rad, n_az, fields, shifts):
    comps, rows, polar, cells = fields.shape
    vmem = pl.BlockSpec(memory_space=pltpu.VMEM)
    tiles = -(-comps * rows // PER_TILE)
    f32 = functools.partial(jax.ShapeDtypeStruct, dtype=jnp.float32)
    low, up, edges = pl.pallas_call(
        functools.partial(halo_kernel, n_rad, n_az),
        out_shape=(f32(fields.shape), f32(fields.shape), f32((6, tiles, polar, LANES))),
        in_specs=[vmem],
        out_specs=(vmem, vmem, vmem),
        scratch_shapes=[
            pltpu.VMEM((2, tiles, polar, LANES), jnp.float32),
            pltpu.SemaphoreType.DMA((8,)),
            pltpu.SemaphoreType.DMA((8,)),
        ],
        compiler_params=pltpu.CompilerParams(collective_id=0, has_side_effects=True),
        name="halo",
    )(fields)
    width = cells + LANES
    count = -(-rows * comps // 8) * 8
    stage_scratch = [
        pltpu.VMEM((comps, rows + 2 * DEEP, polar, width), jnp.float32),
        pltpu.VMEM((comps, rows + DEEP, polar, width), jnp.float32),
        pltpu.VMEM((comps, rows + DEEP, polar, cells), jnp.float32),
        pltpu.VMEM((3, comps, polar, width), jnp.float32),
        pltpu.VMEM((3, comps, polar, width), jnp.float32),
    ]
    if n_az == 4:
        share = count // n_az
        return pl.pallas_call(
            functools.partial(quarter_turn_kernel, n_rad, n_az),
            out_shape=f32(fields.shape),
            in_specs=[vmem] * 4 + [pl.BlockSpec(memory_space=pltpu.SMEM)],
            out_specs=vmem,
            scratch_shapes=[
                pltpu.VMEM((n_az - 1, share, polar, cells), jnp.float32),
                pltpu.VMEM((n_az, share, polar, cells), jnp.float32),
                pltpu.VMEM((count, polar, cells), jnp.float32),
                pltpu.SemaphoreType.DMA((2 * n_az - 2,)),
                pltpu.SemaphoreType.DMA((2 * n_az - 2,)),
                pltpu.VMEM((count, polar, cells), jnp.float32),
                *stage_scratch,
            ],
            compiler_params=pltpu.CompilerParams(
                collective_id=1, has_side_effects=True, vmem_limit_bytes=32 * 1024 * 1024
            ),
            name="stages_turn",
        )(fields, low, up, edges, shifts)
    planes = pl.pallas_call(
        functools.partial(stage_kernel, n_rad),
        out_shape=f32((count, polar, cells)),
        in_specs=[vmem] * 4,
        out_specs=vmem,
        scratch_shapes=stage_scratch,
        compiler_params=pltpu.CompilerParams(vmem_limit_bytes=32 * 1024 * 1024),
        name="stages",
    )(fields, low, up, edges)
    return pl.pallas_call(
        functools.partial(turn_kernel, n_az),
        out_shape=f32(fields.shape),
        in_specs=[vmem, pl.BlockSpec(memory_space=pltpu.SMEM)],
        out_specs=vmem,
        scratch_shapes=[
            pltpu.VMEM((REACH, count, polar, cells), jnp.float32),
            pltpu.SemaphoreType.DMA((REACH,)),
            pltpu.SemaphoreType.DMA((REACH,)),
        ],
        compiler_params=pltpu.CompilerParams(collective_id=1, has_side_effects=True),
        name="turn",
    )(planes, shifts)


def solution(mesh):
    return jax.shard_map(
        functools.partial(on_device, mesh.shape["rad"], mesh.shape["az"]),
        mesh=mesh,
        in_specs=(P(None, "rad", None, "az"), P("rad")),
        out_specs=P(None, "rad", None, "az"),
        check_vma=False,
    )
```

```python
import functools

import jax
import jax.numpy as jnp
from jax import lax
from jax.experimental import pallas as pl
from jax.experimental.pallas import tpu as pltpu
from jax.sharding import PartitionSpec as P

ADIABATIC = 1.4
COURANT_RADIAL = 0.09
COURANT_POLAR = 0.08
COURANT_AZIMUTH = 0.18
MESH = pl.DeviceIdType.MESH
LANES = 128
DEEP = 6
SLOT = 8
PER_TILE = LANES // SLOT
REACH = 3


def pack_edges(block_ref, pack_ref, side):
    comps, rows, polar, cells = block_ref.shape
    lane = lax.broadcasted_iota(jnp.int32, (polar, LANES), 1) // SLOT
    start = 0 if side == 0 else cells - LANES
    for tile in range(pack_ref.shape[1]):
        total = jnp.zeros((polar, LANES), jnp.float32)
        for slot in range(PER_TILE):
            plane = tile * PER_TILE + slot
            if plane < comps * rows:
                part = block_ref[plane // rows, plane % rows, :, start : start + LANES]
                amount = (slot * SLOT + (0 if side == 0 else SLOT)) % LANES
                if amount:
                    part = pltpu.roll(part, amount, 1)
                total = jnp.where(lane == slot, part, total)
        pack_ref[side, tile] = total


def halo_kernel(
    n_rad, n_az, block_ref, low_ref, up_ref, edge_ref, pack_ref, send_sem, recv_sem, farther=()
):
    rad, az = lax.axis_index("rad"), lax.axis_index("az")
    right, left = lax.rem(az + 1, n_az), lax.rem(az + n_az - 1, n_az)
    has = {-1: rad > 0, 1: rad < n_rad - 1}

    def when(step, work):
        if step == 0:
            work()
        else:
            pl.when(has[step])(work)

    barrier = pltpu.get_barrier_semaphore()

    def greet(step):
        def work():
            for column in (left, right) if step == 0 else (az, left, right):
                pl.semaphore_signal(
                    barrier, inc=1, device_id={"rad": rad + step, "az": column}, device_id_type=MESH
                )

        return work

    for step in (0, -1, 1):
        when(step, greet(step))
    for d in farther:
        pl.semaphore_signal(
            barrier, inc=1, device_id={"rad": rad, "az": lax.rem(az + d, n_az)}, device_id_type=MESH
        )
    inside = jnp.logical_and(has[-1], has[1])
    near = jnp.where(inside, 8, 5 if n_rad > 1 else 2)
    pl.semaphore_wait(barrier, near + len(farther))

    def radial(step):
        return pltpu.make_async_remote_copy(
            src_ref=block_ref,
            dst_ref=up_ref if step < 0 else low_ref,
            send_sem=send_sem.at[0 if step < 0 else 1],
            recv_sem=recv_sem.at[0 if step < 0 else 1],
            device_id={"rad": rad + step, "az": az},
            device_id_type=MESH,
        )

    def edge(step, side):
        slot = side * 3 + 1 - step
        return pltpu.make_async_remote_copy(
            src_ref=pack_ref.at[side],
            dst_ref=edge_ref.at[slot],
            send_sem=send_sem.at[2 + slot],
            recv_sem=recv_sem.at[2 + slot],
            device_id={"rad": rad + step, "az": left if side == 0 else right},
            device_id_type=MESH,
        )

    for step in (-1, 1):
        when(step, lambda step=step: radial(step).start())
    for side in (0, 1):
        pack_edges(block_ref, pack_ref, side)
        for step in (0, -1, 1):
            when(step, lambda step=step, side=side: edge(step, side).start())
    for side in (0, 1):
        for step in (0, -1, 1):
            when(step, lambda step=step, side=side: edge(step, side).wait_send())
            when(-step, lambda step=step, side=side: edge(step, side).wait_recv())
    for step in (-1, 1):
        when(step, lambda step=step: radial(step).wait_send())
        when(-step, lambda step=step: radial(step).wait_recv())


def interface(before, centre, follow, beyond):
    value = 7.0 / 12.0 * (centre + follow) - 1.0 / 12.0 * (before + beyond)
    return jnp.clip(value, jnp.minimum(centre, follow), jnp.maximum(centre, follow))


def limited(u, left, right):
    flat = (right - u) * (u - left) <= 0.0
    spread = right - left
    middle = u - 0.5 * (left + right)
    product = spread * middle
    sixth = spread * spread * (1.0 / 6.0)
    triple = 3.0 * u
    new_left = jnp.where(flat, u, jnp.where(product > sixth, triple - 2.0 * right, left))
    new_right = jnp.where(flat, u, jnp.where(product < -sixth, triple - 2.0 * left, right))
    return new_left, new_right


def hllc(left, right, normal):
    gas_left, gas_right = ADIABATIC * left[4], ADIABATIC * right[4]
    sound_left = gas_left * lax.rsqrt(gas_left * left[0])
    sound_right = gas_right * lax.rsqrt(gas_right * right[0])
    u_left, u_right = left[normal], right[normal]
    slow = jnp.minimum(u_left - sound_left, u_right - sound_right)
    fast = jnp.maximum(u_left + sound_left, u_right + sound_right)
    mass_left = left[0] * (u_left - slow)
    mass_right = right[0] * (fast - u_right)
    contact = (mass_left * u_left + mass_right * u_right + left[4] - right[4]) / (
        mass_left + mass_right
    )
    supersonic = slow >= 0.0
    from_left = jnp.logical_or(supersonic, contact >= 0.0)
    rho, v1, v2, v3, p = [jnp.where(from_left, a, b) for a, b in zip(left, right)]
    speeds = (None, v1, v2, v3)
    u = speeds[normal]
    wave = jnp.where(from_left, slow, fast)
    star = jnp.logical_and(slow < 0.0, jnp.logical_or(from_left, fast > 0.0))
    energy = p * (1.0 / (ADIABATIC - 1.0)) + 0.5 * rho * (v1 * v1 + v2 * v2 + v3 * v3)
    momentum = rho * u
    relative = wave - u
    mass = rho * relative
    inverse = 1.0 / (wave - contact)
    factor = mass * inverse
    star_energy = inverse * (relative * energy + (contact - u) * (mass * contact + p))
    flux_mass = momentum + jnp.where(star, wave * (factor - rho), 0.0)
    flux_normal = momentum * u + p + jnp.where(star, wave * (factor * contact - momentum), 0.0)
    flux_energy = (energy + p) * u + jnp.where(star, wave * (star_energy - energy), 0.0)
    out = [flux_mass, None, None, None, flux_energy]
    for axis in (1, 2, 3):
        out[axis] = flux_normal if axis == normal else speeds[axis] * flux_mass
    return out


def conserved_of(w):
    energy = w[4] * (1.0 / (ADIABATIC - 1.0)) + 0.5 * w[0] * (
        w[1] * w[1] + w[2] * w[2] + w[3] * w[3]
    )
    return [w[0], w[0] * w[1], w[0] * w[2], w[0] * w[3], energy]


def primitive_of(u):
    inverse = 1.0 / u[0]
    v = [inverse * u[k] for k in (1, 2, 3)]
    squared = v[0] * v[0] + v[1] * v[1] + v[2] * v[2]
    return [u[0]] + v + [(ADIABATIC - 1.0) * (u[4] - 0.5 * u[0] * squared)]


def rolled(x, amount, axis):
    return pltpu.roll(x, amount % x.shape[axis], axis)


def azimuth_difference(w):
    lows, highs = [], []
    for u in w:
        edge = interface(rolled(u, 1, 1), u, rolled(u, -1, 1), rolled(u, -2, 1))
        low, high = limited(u, rolled(edge, 1, 1), edge)
        lows.append(low)
        highs.append(rolled(high, 1, 1))
    flux = hllc(highs, lows, 3)
    return [rolled(f, -1, 1) - f for f in flux]


def polar_difference(w):
    count = w[0].shape[0]
    place = lax.broadcasted_iota(jnp.int32, w[0].shape, 0)
    first, last = place == 0, place == count - 1
    beyond_last = place >= count - 2
    lows, highs = [], []
    for u in w:
        before = jnp.where(first, u, rolled(u, 1, 0))
        follow = jnp.where(last, u, rolled(u, -1, 0))
        beyond = jnp.where(beyond_last, jnp.where(last, u, follow), rolled(u, -2, 0))
        edge = interface(before, u, follow, beyond)
        low, high = limited(u, jnp.where(first, u, rolled(edge, 1, 0)), edge)
        lows.append(low)
        highs.append(jnp.where(first, u, rolled(high, 1, 0)))
    flux = hllc(highs, lows, 2)
    rho, v1, v2, v3, p = w
    momentum = rho * v2
    energy = conserved_of(w)[4]
    outer = [momentum, momentum * v1, momentum * v2 + p, momentum * v3, (energy + p) * v2]
    return [jnp.where(last, o, rolled(f, -1, 0)) - f for f, o in zip(flux, outer)]


def row_of(ref, row, width):
    return [ref[c, row, :, :width] for c in range(5)]


def radial_start(src, cell, width, keep):
    w = [row_of(src, cell + k, width) for k in (-2, -1, 0, 1, 2)]
    for c in range(5):
        below = interface(*(w[k][c] for k in (0, 1, 2, 3)))
        above = interface(*(w[k][c] for k in (1, 2, 3, 4)))
        keep[0, c, :, :width] = above
        keep[1, c, :, :width] = limited(w[2][c], below, above)[1]


def radial_face(src, cell, width, keep):
    w = [row_of(src, cell + k, width) for k in (0, 1, 2, 3)]
    highs, lows = [], []
    for c in range(5):
        below = keep[0, c, :, :width]
        above = interface(*(w[k][c] for k in (0, 1, 2, 3)))
        low, high = limited(w[1][c], below, above)
        highs.append(keep[1, c, :, :width])
        lows.append(low)
        keep[0, c, :, :width] = above
        keep[1, c, :, :width] = high
    return hllc(highs, lows, 1)


def stage_begin(src, cell, width, keep):
    radial_start(src, cell - 1, width, keep)
    flux = radial_face(src, cell - 1, width, keep)
    for c in range(5):
        keep[2, c, :, :width] = flux[c]


def stage_row(src, cell, width, keep, courant):
    upper = radial_face(src, cell, width, keep)
    total = []
    for c in range(5):
        total.append(COURANT_RADIAL * (upper[c] - keep[2, c, :, :width]))
        keep[2, c, :, :width] = upper[c]
    w = row_of(src, cell, width)
    for c, d in enumerate(polar_difference(w)):
        total[c] += COURANT_POLAR * d
    for c, d in enumerate(azimuth_difference(row_of(src, cell, src.shape[3]))):
        total[c] += courant * d[:, :width]
    return total


def stage_kernel(
    n_rad, block_ref, low_ref, up_ref, edge_ref, out_ref, wide_ref, first_ref, half_ref, keep1, keep2,
    after=None,
):
    comps, rows, polar, cells = block_ref.shape
    rad = lax.axis_index("rad")
    total_rows = rows * n_rad
    lane = lax.broadcasted_iota(jnp.int32, (polar, LANES), 1)

    is_first, is_last = rad == 0, rad == n_rad - 1
    for c in range(comps):
        for r in range(rows):
            wide_ref[c, DEEP + r, :, :cells] = block_ref[c, r]
        for r in range(DEEP):
            wide_ref[c, r, :, :cells] = jnp.where(is_first, block_ref[c, 0], low_ref[c, rows - DEEP + r])
            wide_ref[c, DEEP + rows + r, :, :cells] = jnp.where(
                is_last, block_ref[c, rows - 1], up_ref[c, r]
            )

    def unpacked(which, c, r):
        plane = c * rows + r
        tile, slot = plane // PER_TILE, plane % PER_TILE
        after = rolled(edge_ref[which, tile], -slot * SLOT, 1)
        before = rolled(edge_ref[3 + which, tile], -(slot * SLOT + SLOT), 1)
        return jnp.where(lane < SLOT, after, before)

    for c in range(comps):
        own = [unpacked(1, c, r) for r in range(rows)]
        for r in range(rows):
            wide_ref[c, DEEP + r, :, cells:] = own[r]
        for r in range(DEEP):
            wide_ref[c, r, :, cells:] = jnp.where(is_first, own[0], unpacked(0, c, rows - DEEP + r))
            wide_ref[c, DEEP + rows + r, :, cells:] = jnp.where(is_last, own[rows - 1], unpacked(2, c, r))

    def courant_of(row):
        index = jnp.full((1, 1), rad * rows + row, jnp.int32).astype(jnp.float32)
        return COURANT_AZIMUTH / (1.0 + (index + 0.5) / total_rows)

    width = cells + LANES
    stage_begin(wide_ref, 3, width, keep1)

    def first_row(k, carry):
        change = stage_row(wide_ref, k + 3, width, keep1, courant_of(k - 3))
        start = conserved_of(row_of(wide_ref, k + 3, width))
        new = [a - b for a, b in zip(start, change)]
        w = primitive_of(new)
        for c in range(comps):
            first_ref[c, k, :, :] = w[c]
            half_ref[c, k, :, :] = (0.5 * start[c] + 0.5 * new[c])[:, :cells]
        return carry

    lax.fori_loop(0, rows + 6, first_row, 0)

    @pl.when(is_first)
    def _():
        for r in range(3):
            first_ref[:, r] = first_ref[:, 3]

    @pl.when(is_last)
    def _():
        for r in range(3):
            first_ref[:, rows + 3 + r] = first_ref[:, rows + 2]

    for spare in range(rows * comps, out_ref.shape[0]):
        out_ref[spare] = jnp.zeros((polar, cells), jnp.float32)
    stage_begin(first_ref, 3, cells, keep2)

    def second_row(i, carry):
        change = stage_row(first_ref, i + 3, cells, keep2, courant_of(i))
        w = primitive_of([half_ref[c, i + 3] - 0.5 * change[c] for c in range(comps)])
        for c in range(comps):
            out_ref[i * comps + c] = w[c]
        if after is not None:
            after(i)
        return carry

    lax.fori_loop(0, rows, second_row, 0)


def turn_kernel(n_az, planes_ref, shifts_ref, out_ref, far_ref, send_sem, recv_sem):
    rad, az = lax.axis_index("rad"), lax.axis_index("az")
    comps, rows, polar, cells = out_ref.shape
    barrier = pltpu.get_barrier_semaphore()
    for d in range(1, REACH + 1):
        for column in (lax.rem(az + d, n_az), lax.rem(az + n_az - d, n_az)):
            pl.semaphore_signal(
                barrier, inc=1, device_id={"rad": rad, "az": column}, device_id_type=MESH
            )
    pl.semaphore_wait(barrier, 2 * REACH)

    def send(d):
        return pltpu.make_async_remote_copy(
            src_ref=planes_ref,
            dst_ref=far_ref.at[d - 1],
            send_sem=send_sem.at[d - 1],
            recv_sem=recv_sem.at[d - 1],
            device_id={"rad": rad, "az": lax.rem(az + d, n_az)},
            device_id_type=MESH,
        )

    for d in range(1, REACH + 1):
        send(d).start()
    for d in range(1, REACH + 1):
        send(d).wait()
    lane = lax.broadcasted_iota(jnp.int32, (polar, cells), 1)
    for i in range(rows):
        amount = shifts_ref[i]
        quotient = amount // cells
        rest = amount - quotient * cells
        for c in range(comps):
            blocks = [planes_ref[i * comps + c]] + [far_ref[d, i * comps + c] for d in range(REACH)]
            near, far = blocks[0], blocks[1]
            for d in range(1, REACH + 1):
                near = jnp.where(quotient == d, blocks[d], near)
                if d < REACH:
                    far = jnp.where(quotient == d, blocks[d + 1], far)
            out_ref[c, i] = pltpu.roll(jnp.where(lane >= cells - rest, far, near), rest, 1)


def quarter_turn_kernel(
    n_rad, n_az, block_ref, shifts_ref, out_ref, low_ref, up_ref, edge_ref, pack_ref, halo_send,
    halo_recv, far_ref, turned_ref, back_ref, send_sem, recv_sem, planes_ref, *stage_refs
):
    rad, az = lax.axis_index("rad"), lax.axis_index("az")
    comps, rows, polar, cells = out_ref.shape
    share = planes_ref.shape[0] // n_az
    halo_kernel(
        n_rad, n_az, block_ref, low_ref, up_ref, edge_ref, pack_ref, halo_send, halo_recv,
        tuple(range(2, n_az - 1)),
    )

    def gather(d):
        owner = lax.rem(az + d, n_az)
        return pltpu.make_async_remote_copy(
            src_ref=planes_ref.at[pl.ds(owner * share, share)],
            dst_ref=far_ref.at[d - 1],
            send_sem=send_sem.at[d - 1],
            recv_sem=recv_sem.at[d - 1],
            device_id={"rad": rad, "az": owner},
            device_id_type=MESH,
        )

    def home(g):
        return pltpu.make_async_remote_copy(
            src_ref=turned_ref.at[g],
            dst_ref=back_ref.at[pl.ds(az * share, share)],
            send_sem=send_sem.at[n_az - 2 + g],
            recv_sem=recv_sem.at[n_az - 2 + g],
            device_id={"rad": rad, "az": lax.rem(az + g, n_az)},
            device_id_type=MESH,
        )

    def after(i):
        for owner in range(n_az):
            last = (min((owner + 1) * share, rows * comps) - 1) // comps
            d = lax.rem(owner - az + n_az, n_az)

            @pl.when(jnp.logical_and(i == last, az != owner))
            def _(owner=owner, d=d):
                pltpu.make_async_remote_copy(
                    src_ref=planes_ref.at[pl.ds(owner * share, share)],
                    dst_ref=far_ref.at[d - 1],
                    send_sem=send_sem.at[d - 1],
                    recv_sem=recv_sem.at[d - 1],
                    device_id={"rad": rad, "az": owner},
                    device_id_type=MESH,
                ).start()

    stage_kernel(
        n_rad, block_ref, low_ref, up_ref, edge_ref, planes_ref, *stage_refs, after=after
    )
    for d in range(1, n_az):
        gather(d).wait()
    lane = lax.broadcasted_iota(jnp.int32, (polar, cells), 1)
    for k in range(share):
        row = jnp.minimum((az * share + k) // comps, rows - 1)
        amount = shifts_ref[row]
        quotient = amount // cells
        rest = amount - quotient * cells
        blocks = [planes_ref[az * share + k]] + [far_ref[d, k] for d in range(n_az - 1)]
        blocks = [pltpu.roll(b, rest, 1) for b in blocks]
        ahead = blocks
        for q in range(1, n_az):
            ahead = [
                jnp.where(quotient == q, blocks[(q + j) % n_az], a) for j, a in enumerate(ahead)
            ]
        for g in range(n_az):
            turned = jnp.where(lane < rest, ahead[(1 - g) % n_az], ahead[-g % n_az])
            if g:
                turned_ref[g, k] = turned
            else:
                back_ref[az * share + k] = turned
    for g in range(1, n_az):
        home(g).start()
    for g in range(1, n_az):
        home(g).wait_send()
        sender = lax.rem(az + n_az - g, n_az)
        pltpu.make_async_remote_copy(
            src_ref=turned_ref.at[g],
            dst_ref=back_ref.at[pl.ds(sender * share, share)],
            send_sem=send_sem.at[n_az - 2 + g],
            recv_sem=recv_sem.at[n_az - 2 + g],
            device_id={"rad": rad, "az": lax.rem(az + g, n_az)},
            device_id_type=MESH,
        ).wait_recv()
    for i in range(rows):
        for c in range(comps):
            out_ref[c, i] = back_ref[i * comps + c]


def on_device(n_rad, n_az, fields, shifts):
    comps, rows, polar, cells = fields.shape
    vmem = pl.BlockSpec(memory_space=pltpu.VMEM)
    tiles = -(-comps * rows // PER_TILE)
    f32 = functools.partial(jax.ShapeDtypeStruct, dtype=jnp.float32)
    width = cells + LANES
    count = -(-rows * comps // 8) * 8
    stage_scratch = [
        pltpu.VMEM((comps, rows + 2 * DEEP, polar, width), jnp.float32),
        pltpu.VMEM((comps, rows + DEEP, polar, width), jnp.float32),
        pltpu.VMEM((comps, rows + DEEP, polar, cells), jnp.float32),
        pltpu.VMEM((3, comps, polar, width), jnp.float32),
        pltpu.VMEM((3, comps, polar, width), jnp.float32),
    ]
    if n_az == 4:
        share = count // n_az
        return pl.pallas_call(
            functools.partial(quarter_turn_kernel, n_rad, n_az),
            out_shape=f32(fields.shape),
            in_specs=[vmem, pl.BlockSpec(memory_space=pltpu.SMEM)],
            out_specs=vmem,
            scratch_shapes=[
                pltpu.VMEM(fields.shape, jnp.float32),
                pltpu.VMEM(fields.shape, jnp.float32),
                pltpu.VMEM((6, tiles, polar, LANES), jnp.float32),
                pltpu.VMEM((2, tiles, polar, LANES), jnp.float32),
                pltpu.SemaphoreType.DMA((8,)),
                pltpu.SemaphoreType.DMA((8,)),
                pltpu.VMEM((n_az - 1, share, polar, cells), jnp.float32),
                pltpu.VMEM((n_az, share, polar, cells), jnp.float32),
                pltpu.VMEM((count, polar, cells), jnp.float32),
                pltpu.SemaphoreType.DMA((2 * n_az - 2,)),
                pltpu.SemaphoreType.DMA((2 * n_az - 2,)),
                pltpu.VMEM((count, polar, cells), jnp.float32),
                *stage_scratch,
            ],
            compiler_params=pltpu.CompilerParams(
                collective_id=1, has_side_effects=True, vmem_limit_bytes=32 * 1024 * 1024
            ),
            name="whole_step",
        )(fields, shifts)
    low, up, edges = pl.pallas_call(
        functools.partial(halo_kernel, n_rad, n_az),
        out_shape=(f32(fields.shape), f32(fields.shape), f32((6, tiles, polar, LANES))),
        in_specs=[vmem],
        out_specs=(vmem, vmem, vmem),
        scratch_shapes=[
            pltpu.VMEM((2, tiles, polar, LANES), jnp.float32),
            pltpu.SemaphoreType.DMA((8,)),
            pltpu.SemaphoreType.DMA((8,)),
        ],
        compiler_params=pltpu.CompilerParams(collective_id=0, has_side_effects=True),
        name="halo",
    )(fields)
    planes = pl.pallas_call(
        functools.partial(stage_kernel, n_rad),
        out_shape=f32((count, polar, cells)),
        in_specs=[vmem] * 4,
        out_specs=vmem,
        scratch_shapes=stage_scratch,
        compiler_params=pltpu.CompilerParams(vmem_limit_bytes=32 * 1024 * 1024),
        name="stages",
    )(fields, low, up, edges)
    return pl.pallas_call(
        functools.partial(turn_kernel, n_az),
        out_shape=f32(fields.shape),
        in_specs=[vmem, pl.BlockSpec(memory_space=pltpu.SMEM)],
        out_specs=vmem,
        scratch_shapes=[
            pltpu.VMEM((REACH, count, polar, cells), jnp.float32),
            pltpu.SemaphoreType.DMA((REACH,)),
            pltpu.SemaphoreType.DMA((REACH,)),
        ],
        compiler_params=pltpu.CompilerParams(collective_id=1, has_side_effects=True),
        name="turn",
    )(planes, shifts)


def solution(mesh):
    return jax.shard_map(
        functools.partial(on_device, mesh.shape["rad"], mesh.shape["az"]),
        mesh=mesh,
        in_specs=(P(None, "rad", None, "az"), P("rad")),
        out_specs=P(None, "rad", None, "az"),
        check_vma=False,
    )
```

```python
import functools

import jax
import jax.numpy as jnp
from jax import lax
from jax.experimental import pallas as pl
from jax.experimental.pallas import tpu as pltpu
from jax.sharding import PartitionSpec as P

ADIABATIC = 1.4
COURANT_RADIAL = 0.09
COURANT_POLAR = 0.08
COURANT_AZIMUTH = 0.18
MESH = pl.DeviceIdType.MESH
LANES = 128
DEEP = 6
SLOT = 8
PER_TILE = LANES // SLOT
REACH = 3


def pack_edges(block_ref, pack_ref, side):
    comps, rows, polar, cells = block_ref.shape
    lane = lax.broadcasted_iota(jnp.int32, (polar, LANES), 1) // SLOT
    start = 0 if side == 0 else cells - LANES
    for tile in range(pack_ref.shape[1]):
        total = jnp.zeros((polar, LANES), jnp.float32)
        for slot in range(PER_TILE):
            plane = tile * PER_TILE + slot
            if plane < comps * rows:
                part = block_ref[plane // rows, plane % rows, :, start : start + LANES]
                amount = (slot * SLOT + (0 if side == 0 else SLOT)) % LANES
                if amount:
                    part = pltpu.roll(part, amount, 1)
                total = jnp.where(lane == slot, part, total)
        pack_ref[side, tile] = total


def halo_kernel(
    n_rad, n_az, block_ref, low_ref, up_ref, edge_ref, pack_ref, send_sem, recv_sem, farther=(),
    between=None,
):
    rad, az = lax.axis_index("rad"), lax.axis_index("az")
    right, left = lax.rem(az + 1, n_az), lax.rem(az + n_az - 1, n_az)
    has = {-1: rad > 0, 1: rad < n_rad - 1}

    def when(step, work):
        if step == 0:
            work()
        else:
            pl.when(has[step])(work)

    barrier = pltpu.get_barrier_semaphore()

    def greet(step):
        def work():
            for column in (left, right) if step == 0 else (az, left, right):
                pl.semaphore_signal(
                    barrier, inc=1, device_id={"rad": rad + step, "az": column}, device_id_type=MESH
                )

        return work

    for step in (0, -1, 1):
        when(step, greet(step))
    for d in farther:
        pl.semaphore_signal(
            barrier, inc=1, device_id={"rad": rad, "az": lax.rem(az + d, n_az)}, device_id_type=MESH
        )
    inside = jnp.logical_and(has[-1], has[1])
    near = jnp.where(inside, 8, 5 if n_rad > 1 else 2)
    pl.semaphore_wait(barrier, near + len(farther))

    def radial(step):
        return pltpu.make_async_remote_copy(
            src_ref=block_ref,
            dst_ref=up_ref if step < 0 else low_ref,
            send_sem=send_sem.at[0 if step < 0 else 1],
            recv_sem=recv_sem.at[0 if step < 0 else 1],
            device_id={"rad": rad + step, "az": az},
            device_id_type=MESH,
        )

    def edge(step, side):
        slot = side * 3 + 1 - step
        return pltpu.make_async_remote_copy(
            src_ref=pack_ref.at[side],
            dst_ref=edge_ref.at[slot],
            send_sem=send_sem.at[2 + slot],
            recv_sem=recv_sem.at[2 + slot],
            device_id={"rad": rad + step, "az": left if side == 0 else right},
            device_id_type=MESH,
        )

    for step in (-1, 1):
        when(step, lambda step=step: radial(step).start())
    for side in (0, 1):
        pack_edges(block_ref, pack_ref, side)
        for step in (0, -1, 1):
            when(step, lambda step=step, side=side: edge(step, side).start())
    for side in (0, 1):
        edge(0, side).wait_recv()
    if between is not None:
        between()
    for side in (0, 1):
        edge(0, side).wait_send()
        for step in (-1, 1):
            when(step, lambda step=step, side=side: edge(step, side).wait_send())
            when(-step, lambda step=step, side=side: edge(step, side).wait_recv())
    for step in (-1, 1):
        when(step, lambda step=step: radial(step).wait_send())
        when(-step, lambda step=step: radial(step).wait_recv())


def interface(before, centre, follow, beyond):
    value = 7.0 / 12.0 * (centre + follow) - 1.0 / 12.0 * (before + beyond)
    return jnp.clip(value, jnp.minimum(centre, follow), jnp.maximum(centre, follow))


def limited(u, left, right):
    flat = (right - u) * (u - left) <= 0.0
    spread = right - left
    middle = u - 0.5 * (left + right)
    product = spread * middle
    sixth = spread * spread * (1.0 / 6.0)
    triple = 3.0 * u
    new_left = jnp.where(flat, u, jnp.where(product > sixth, triple - 2.0 * right, left))
    new_right = jnp.where(flat, u, jnp.where(product < -sixth, triple - 2.0 * left, right))
    return new_left, new_right


def hllc(left, right, normal):
    gas_left, gas_right = ADIABATIC * left[4], ADIABATIC * right[4]
    sound_left = gas_left * lax.rsqrt(gas_left * left[0])
    sound_right = gas_right * lax.rsqrt(gas_right * right[0])
    u_left, u_right = left[normal], right[normal]
    slow = jnp.minimum(u_left - sound_left, u_right - sound_right)
    fast = jnp.maximum(u_left + sound_left, u_right + sound_right)
    mass_left = left[0] * (u_left - slow)
    mass_right = right[0] * (fast - u_right)
    contact = (mass_left * u_left + mass_right * u_right + left[4] - right[4]) / (
        mass_left + mass_right
    )
    supersonic = slow >= 0.0
    from_left = jnp.logical_or(supersonic, contact >= 0.0)
    rho, v1, v2, v3, p = [jnp.where(from_left, a, b) for a, b in zip(left, right)]
    speeds = (None, v1, v2, v3)
    u = speeds[normal]
    wave = jnp.where(from_left, slow, fast)
    star = jnp.logical_and(slow < 0.0, jnp.logical_or(from_left, fast > 0.0))
    energy = p * (1.0 / (ADIABATIC - 1.0)) + 0.5 * rho * (v1 * v1 + v2 * v2 + v3 * v3)
    momentum = rho * u
    relative = wave - u
    mass = rho * relative
    inverse = 1.0 / (wave - contact)
    factor = mass * inverse
    star_energy = inverse * (relative * energy + (contact - u) * (mass * contact + p))
    flux_mass = momentum + jnp.where(star, wave * (factor - rho), 0.0)
    flux_normal = momentum * u + p + jnp.where(star, wave * (factor * contact - momentum), 0.0)
    flux_energy = (energy + p) * u + jnp.where(star, wave * (star_energy - energy), 0.0)
    out = [flux_mass, None, None, None, flux_energy]
    for axis in (1, 2, 3):
        out[axis] = flux_normal if axis == normal else speeds[axis] * flux_mass
    return out


def conserved_of(w):
    energy = w[4] * (1.0 / (ADIABATIC - 1.0)) + 0.5 * w[0] * (
        w[1] * w[1] + w[2] * w[2] + w[3] * w[3]
    )
    return [w[0], w[0] * w[1], w[0] * w[2], w[0] * w[3], energy]


def primitive_of(u):
    inverse = 1.0 / u[0]
    v = [inverse * u[k] for k in (1, 2, 3)]
    squared = v[0] * v[0] + v[1] * v[1] + v[2] * v[2]
    return [u[0]] + v + [(ADIABATIC - 1.0) * (u[4] - 0.5 * u[0] * squared)]


def rolled(x, amount, axis):
    return pltpu.roll(x, amount % x.shape[axis], axis)


def azimuth_difference(w):
    lows, highs = [], []
    for u in w:
        edge = interface(rolled(u, 1, 1), u, rolled(u, -1, 1), rolled(u, -2, 1))
        low, high = limited(u, rolled(edge, 1, 1), edge)
        lows.append(low)
        highs.append(rolled(high, 1, 1))
    flux = hllc(highs, lows, 3)
    return [rolled(f, -1, 1) - f for f in flux]


def polar_difference(w):
    count = w[0].shape[0]
    place = lax.broadcasted_iota(jnp.int32, w[0].shape, 0)
    first, last = place == 0, place == count - 1
    beyond_last = place >= count - 2
    lows, highs = [], []
    for u in w:
        before = jnp.where(first, u, rolled(u, 1, 0))
        follow = jnp.where(last, u, rolled(u, -1, 0))
        beyond = jnp.where(beyond_last, jnp.where(last, u, follow), rolled(u, -2, 0))
        edge = interface(before, u, follow, beyond)
        low, high = limited(u, jnp.where(first, u, rolled(edge, 1, 0)), edge)
        lows.append(low)
        highs.append(jnp.where(first, u, rolled(high, 1, 0)))
    flux = hllc(highs, lows, 2)
    rho, v1, v2, v3, p = w
    momentum = rho * v2
    energy = conserved_of(w)[4]
    outer = [momentum, momentum * v1, momentum * v2 + p, momentum * v3, (energy + p) * v2]
    return [jnp.where(last, o, rolled(f, -1, 0)) - f for f, o in zip(flux, outer)]


def row_of(ref, row, width):
    return [ref[c, row, :, :width] for c in range(5)]


def radial_start(src, cell, width, keep):
    w = [row_of(src, cell + k, width) for k in (-2, -1, 0, 1, 2)]
    for c in range(5):
        below = interface(*(w[k][c] for k in (0, 1, 2, 3)))
        above = interface(*(w[k][c] for k in (1, 2, 3, 4)))
        keep[0, c, :, :width] = above
        keep[1, c, :, :width] = limited(w[2][c], below, above)[1]


def radial_face(src, cell, width, keep):
    w = [row_of(src, cell + k, width) for k in (0, 1, 2, 3)]
    highs, lows = [], []
    for c in range(5):
        below = keep[0, c, :, :width]
        above = interface(*(w[k][c] for k in (0, 1, 2, 3)))
        low, high = limited(w[1][c], below, above)
        highs.append(keep[1, c, :, :width])
        lows.append(low)
        keep[0, c, :, :width] = above
        keep[1, c, :, :width] = high
    return hllc(highs, lows, 1)


def stage_begin(src, cell, width, keep):
    radial_start(src, cell - 1, width, keep)
    flux = radial_face(src, cell - 1, width, keep)
    for c in range(5):
        keep[2, c, :, :width] = flux[c]


def cross_change(src, cell, width, courant):
    total = [COURANT_POLAR * d for d in polar_difference(row_of(src, cell, width))]
    for c, d in enumerate(azimuth_difference(row_of(src, cell, src.shape[3]))):
        total[c] += courant * d[:, :width]
    return total


def radial_change(src, cell, width, keep):
    upper = radial_face(src, cell, width, keep)
    total = []
    for c in range(5):
        total.append(COURANT_RADIAL * (upper[c] - keep[2, c, :, :width]))
        keep[2, c, :, :width] = upper[c]
    return total


def courant_of(row, rows, n_rad):
    index = jnp.full((1, 1), lax.axis_index("rad") * rows + row, jnp.int32).astype(jnp.float32)
    return COURANT_AZIMUTH / (1.0 + (index + 0.5) / (rows * n_rad))


def unpacked(edge_ref, which, plane):
    lane = lax.broadcasted_iota(jnp.int32, edge_ref.shape[2:], 1)
    tile, slot = plane // PER_TILE, plane % PER_TILE
    after = rolled(edge_ref[which, tile], -slot * SLOT, 1)
    before = rolled(edge_ref[3 + which, tile], -(slot * SLOT + SLOT), 1)
    return jnp.where(lane < SLOT, after, before)


def own_rows(n_rad, block_ref, edge_ref, wide_ref, cross_ref):
    comps, rows, polar, cells = block_ref.shape
    for c in range(comps):
        for r in range(rows):
            wide_ref[c, DEEP + r, :, :cells] = block_ref[c, r]
            wide_ref[c, DEEP + r, :, cells:] = unpacked(edge_ref, 1, c * rows + r)

    def row(r, carry):
        change = cross_change(wide_ref, DEEP + r, cells + LANES, courant_of(r, rows, n_rad))
        for c in range(comps):
            cross_ref[c, r] = change[c]
        return carry

    lax.fori_loop(0, rows, row, 0)


def stage_kernel(
    n_rad, block_ref, low_ref, up_ref, edge_ref, out_ref, wide_ref, first_ref, half_ref, keep1, keep2,
    cross_ref, after=None, own_done=False,
):
    comps, rows, polar, cells = block_ref.shape
    rad = lax.axis_index("rad")
    if not own_done:
        own_rows(n_rad, block_ref, edge_ref, wide_ref, cross_ref)

    is_first, is_last = rad == 0, rad == n_rad - 1
    for c in range(comps):
        bottom, top = wide_ref[c, DEEP, :, cells:], wide_ref[c, DEEP + rows - 1, :, cells:]
        for r in range(DEEP):
            below, above = r, DEEP + rows + r
            low, up = c * rows + rows - DEEP + r, c * rows + r
            wide_ref[c, below, :, :cells] = jnp.where(
                is_first, block_ref[c, 0], low_ref[c, rows - DEEP + r]
            )
            wide_ref[c, above, :, :cells] = jnp.where(is_last, block_ref[c, rows - 1], up_ref[c, r])
            wide_ref[c, below, :, cells:] = jnp.where(is_first, bottom, unpacked(edge_ref, 0, low))
            wide_ref[c, above, :, cells:] = jnp.where(is_last, top, unpacked(edge_ref, 2, up))

    width = cells + LANES
    stage_begin(wide_ref, 3, width, keep1)

    def first_row(k, own):
        if own:
            cross = [cross_ref[c, k - 3] for c in range(comps)]
        else:
            cross = cross_change(wide_ref, k + 3, width, courant_of(k - 3, rows, n_rad))
        radial = radial_change(wide_ref, k + 3, width, keep1)
        start = conserved_of(row_of(wide_ref, k + 3, width))
        new = [a - (b + d) for a, b, d in zip(start, radial, cross)]
        w = primitive_of(new)
        for c in range(comps):
            first_ref[c, k, :, :] = w[c]
            half_ref[c, k, :, :] = (0.5 * start[c] + 0.5 * new[c])[:, :cells]

    for begin, end, own in ((0, 3, False), (3, rows + 3, True), (rows + 3, rows + 6, False)):
        lax.fori_loop(begin, end, lambda k, carry, own=own: (first_row(k, own), carry)[1], 0)

    @pl.when(is_first)
    def _():
        for r in range(3):
            first_ref[:, r] = first_ref[:, 3]

    @pl.when(is_last)
    def _():
        for r in range(3):
            first_ref[:, rows + 3 + r] = first_ref[:, rows + 2]

    for spare in range(rows * comps, out_ref.shape[0]):
        out_ref[spare] = jnp.zeros((polar, cells), jnp.float32)
    stage_begin(first_ref, 3, cells, keep2)

    def second_row(i, carry):
        radial = radial_change(first_ref, i + 3, cells, keep2)
        cross = cross_change(first_ref, i + 3, cells, courant_of(i, rows, n_rad))
        change = [a + b for a, b in zip(radial, cross)]
        w = primitive_of([half_ref[c, i + 3] - 0.5 * change[c] for c in range(comps)])
        for c in range(comps):
            out_ref[i * comps + c] = w[c]
        if after is not None:
            after(i)
        return carry

    lax.fori_loop(0, rows, second_row, 0)


def turn_kernel(n_az, planes_ref, shifts_ref, out_ref, far_ref, send_sem, recv_sem):
    rad, az = lax.axis_index("rad"), lax.axis_index("az")
    comps, rows, polar, cells = out_ref.shape
    barrier = pltpu.get_barrier_semaphore()
    for d in range(1, REACH + 1):
        for column in (lax.rem(az + d, n_az), lax.rem(az + n_az - d, n_az)):
            pl.semaphore_signal(
                barrier, inc=1, device_id={"rad": rad, "az": column}, device_id_type=MESH
            )
    pl.semaphore_wait(barrier, 2 * REACH)

    def send(d):
        return pltpu.make_async_remote_copy(
            src_ref=planes_ref,
            dst_ref=far_ref.at[d - 1],
            send_sem=send_sem.at[d - 1],
            recv_sem=recv_sem.at[d - 1],
            device_id={"rad": rad, "az": lax.rem(az + d, n_az)},
            device_id_type=MESH,
        )

    for d in range(1, REACH + 1):
        send(d).start()
    for d in range(1, REACH + 1):
        send(d).wait()
    lane = lax.broadcasted_iota(jnp.int32, (polar, cells), 1)
    for i in range(rows):
        amount = shifts_ref[i]
        quotient = amount // cells
        rest = amount - quotient * cells
        for c in range(comps):
            blocks = [planes_ref[i * comps + c]] + [far_ref[d, i * comps + c] for d in range(REACH)]
            near, far = blocks[0], blocks[1]
            for d in range(1, REACH + 1):
                near = jnp.where(quotient == d, blocks[d], near)
                if d < REACH:
                    far = jnp.where(quotient == d, blocks[d + 1], far)
            out_ref[c, i] = pltpu.roll(jnp.where(lane >= cells - rest, far, near), rest, 1)


def quarter_turn_kernel(
    n_rad, n_az, block_ref, shifts_ref, out_ref, low_ref, up_ref, edge_ref, pack_ref, halo_send,
    halo_recv, far_ref, turned_ref, back_ref, send_sem, recv_sem, planes_ref, *stage_refs
):
    rad, az = lax.axis_index("rad"), lax.axis_index("az")
    comps, rows, polar, cells = out_ref.shape
    share = planes_ref.shape[0] // n_az
    halo_kernel(
        n_rad, n_az, block_ref, low_ref, up_ref, edge_ref, pack_ref, halo_send, halo_recv,
        tuple(range(2, n_az - 1)),
        lambda: own_rows(n_rad, block_ref, edge_ref, stage_refs[0], stage_refs[-1]),
    )

    def gather(d):
        owner = lax.rem(az + d, n_az)
        return pltpu.make_async_remote_copy(
            src_ref=planes_ref.at[pl.ds(owner * share, share)],
            dst_ref=far_ref.at[d - 1],
            send_sem=send_sem.at[d - 1],
            recv_sem=recv_sem.at[d - 1],
            device_id={"rad": rad, "az": owner},
            device_id_type=MESH,
        )

    def home(g):
        return pltpu.make_async_remote_copy(
            src_ref=turned_ref.at[g],
            dst_ref=back_ref.at[pl.ds(az * share, share)],
            send_sem=send_sem.at[n_az - 2 + g],
            recv_sem=recv_sem.at[n_az - 2 + g],
            device_id={"rad": rad, "az": lax.rem(az + g, n_az)},
            device_id_type=MESH,
        )

    def after(i):
        for owner in range(n_az):
            last = (min((owner + 1) * share, rows * comps) - 1) // comps
            d = lax.rem(owner - az + n_az, n_az)

            @pl.when(jnp.logical_and(i == last, az != owner))
            def _(owner=owner, d=d):
                pltpu.make_async_remote_copy(
                    src_ref=planes_ref.at[pl.ds(owner * share, share)],
                    dst_ref=far_ref.at[d - 1],
                    send_sem=send_sem.at[d - 1],
                    recv_sem=recv_sem.at[d - 1],
                    device_id={"rad": rad, "az": owner},
                    device_id_type=MESH,
                ).start()

    stage_kernel(
        n_rad, block_ref, low_ref, up_ref, edge_ref, planes_ref, *stage_refs, after=after,
        own_done=True,
    )
    for d in range(1, n_az):
        gather(d).wait()
    lane = lax.broadcasted_iota(jnp.int32, (polar, cells), 1)
    for k in range(share):
        row = jnp.minimum((az * share + k) // comps, rows - 1)
        amount = shifts_ref[row]
        quotient = amount // cells
        rest = amount - quotient * cells
        blocks = [planes_ref[az * share + k]] + [far_ref[d, k] for d in range(n_az - 1)]
        blocks = [pltpu.roll(b, rest, 1) for b in blocks]
        ahead = blocks
        for q in range(1, n_az):
            ahead = [
                jnp.where(quotient == q, blocks[(q + j) % n_az], a) for j, a in enumerate(ahead)
            ]
        for g in range(n_az):
            turned = jnp.where(lane < rest, ahead[(1 - g) % n_az], ahead[-g % n_az])
            if g:
                turned_ref[g, k] = turned
            else:
                back_ref[az * share + k] = turned
    for g in range(1, n_az):
        home(g).start()
    for g in range(1, n_az):
        home(g).wait_send()
        sender = lax.rem(az + n_az - g, n_az)
        pltpu.make_async_remote_copy(
            src_ref=turned_ref.at[g],
            dst_ref=back_ref.at[pl.ds(sender * share, share)],
            send_sem=send_sem.at[n_az - 2 + g],
            recv_sem=recv_sem.at[n_az - 2 + g],
            device_id={"rad": rad, "az": lax.rem(az + g, n_az)},
            device_id_type=MESH,
        ).wait_recv()
    for i in range(rows):
        for c in range(comps):
            out_ref[c, i] = back_ref[i * comps + c]


def on_device(n_rad, n_az, fields, shifts):
    comps, rows, polar, cells = fields.shape
    vmem = pl.BlockSpec(memory_space=pltpu.VMEM)
    tiles = -(-comps * rows // PER_TILE)
    f32 = functools.partial(jax.ShapeDtypeStruct, dtype=jnp.float32)
    width = cells + LANES
    count = -(-rows * comps // 8) * 8
    stage_scratch = [
        pltpu.VMEM((comps, rows + 2 * DEEP, polar, width), jnp.float32),
        pltpu.VMEM((comps, rows + DEEP, polar, width), jnp.float32),
        pltpu.VMEM((comps, rows + DEEP, polar, cells), jnp.float32),
        pltpu.VMEM((3, comps, polar, width), jnp.float32),
        pltpu.VMEM((3, comps, polar, width), jnp.float32),
        pltpu.VMEM((comps, rows, polar, width), jnp.float32),
    ]
    if n_az == 4:
        share = count // n_az
        return pl.pallas_call(
            functools.partial(quarter_turn_kernel, n_rad, n_az),
            out_shape=f32(fields.shape),
            in_specs=[vmem, pl.BlockSpec(memory_space=pltpu.SMEM)],
            out_specs=vmem,
            scratch_shapes=[
                pltpu.VMEM(fields.shape, jnp.float32),
                pltpu.VMEM(fields.shape, jnp.float32),
                pltpu.VMEM((6, tiles, polar, LANES), jnp.float32),
                pltpu.VMEM((2, tiles, polar, LANES), jnp.float32),
                pltpu.SemaphoreType.DMA((8,)),
                pltpu.SemaphoreType.DMA((8,)),
                pltpu.VMEM((n_az - 1, share, polar, cells), jnp.float32),
                pltpu.VMEM((n_az, share, polar, cells), jnp.float32),
                pltpu.VMEM((count, polar, cells), jnp.float32),
                pltpu.SemaphoreType.DMA((2 * n_az - 2,)),
                pltpu.SemaphoreType.DMA((2 * n_az - 2,)),
                pltpu.VMEM((count, polar, cells), jnp.float32),
                *stage_scratch,
            ],
            compiler_params=pltpu.CompilerParams(
                collective_id=1, has_side_effects=True, vmem_limit_bytes=32 * 1024 * 1024
            ),
            name="whole_step",
        )(fields, shifts)
    low, up, edges = pl.pallas_call(
        functools.partial(halo_kernel, n_rad, n_az),
        out_shape=(f32(fields.shape), f32(fields.shape), f32((6, tiles, polar, LANES))),
        in_specs=[vmem],
        out_specs=(vmem, vmem, vmem),
        scratch_shapes=[
            pltpu.VMEM((2, tiles, polar, LANES), jnp.float32),
            pltpu.SemaphoreType.DMA((8,)),
            pltpu.SemaphoreType.DMA((8,)),
        ],
        compiler_params=pltpu.CompilerParams(collective_id=0, has_side_effects=True),
        name="halo",
    )(fields)
    planes = pl.pallas_call(
        functools.partial(stage_kernel, n_rad),
        out_shape=f32((count, polar, cells)),
        in_specs=[vmem] * 4,
        out_specs=vmem,
        scratch_shapes=stage_scratch,
        compiler_params=pltpu.CompilerParams(vmem_limit_bytes=32 * 1024 * 1024),
        name="stages",
    )(fields, low, up, edges)
    return pl.pallas_call(
        functools.partial(turn_kernel, n_az),
        out_shape=f32(fields.shape),
        in_specs=[vmem, pl.BlockSpec(memory_space=pltpu.SMEM)],
        out_specs=vmem,
        scratch_shapes=[
            pltpu.VMEM((REACH, count, polar, cells), jnp.float32),
            pltpu.SemaphoreType.DMA((REACH,)),
            pltpu.SemaphoreType.DMA((REACH,)),
        ],
        compiler_params=pltpu.CompilerParams(collective_id=1, has_side_effects=True),
        name="turn",
    )(planes, shifts)


def solution(mesh):
    return jax.shard_map(
        functools.partial(on_device, mesh.shape["rad"], mesh.shape["az"]),
        mesh=mesh,
        in_specs=(P(None, "rad", None, "az"), P("rad")),
        out_specs=P(None, "rad", None, "az"),
        check_vma=False,
    )
```

```python
import functools

import jax
import jax.numpy as jnp
from jax import lax
from jax.experimental import pallas as pl
from jax.experimental.pallas import tpu as pltpu
from jax.sharding import PartitionSpec as P

ADIABATIC = 1.4
COURANT_RADIAL = 0.09
COURANT_POLAR = 0.08
COURANT_AZIMUTH = 0.18
MESH = pl.DeviceIdType.MESH
LANES = 128
DEEP = 6
SLOT = 8
PER_TILE = LANES // SLOT
REACH = 3


def pack_edges(block_ref, pack_ref, side):
    comps, rows, polar, cells = block_ref.shape
    lane = lax.broadcasted_iota(jnp.int32, (polar, LANES), 1) // SLOT
    start = 0 if side == 0 else cells - LANES
    for tile in range(pack_ref.shape[1]):
        total = jnp.zeros((polar, LANES), jnp.float32)
        for slot in range(PER_TILE):
            plane = tile * PER_TILE + slot
            if plane < comps * rows:
                part = block_ref[plane // rows, plane % rows, :, start : start + LANES]
                amount = (slot * SLOT + (0 if side == 0 else SLOT)) % LANES
                if amount:
                    part = pltpu.roll(part, amount, 1)
                total = jnp.where(lane == slot, part, total)
        pack_ref[side, tile] = total


def halo_kernel(
    n_rad, n_az, block_ref, low_ref, up_ref, edge_ref, pack_ref, send_sem, recv_sem, farther=(),
    between=None,
):
    rad, az = lax.axis_index("rad"), lax.axis_index("az")
    right, left = lax.rem(az + 1, n_az), lax.rem(az + n_az - 1, n_az)
    has = {-1: rad > 0, 1: rad < n_rad - 1}

    def when(step, work):
        if step == 0:
            work()
        else:
            pl.when(has[step])(work)

    barrier = pltpu.get_barrier_semaphore()

    def greet(step):
        def work():
            for column in (left, right) if step == 0 else (az, left, right):
                pl.semaphore_signal(
                    barrier, inc=1, device_id={"rad": rad + step, "az": column}, device_id_type=MESH
                )

        return work

    for step in (0, -1, 1):
        when(step, greet(step))
    for d in farther:
        pl.semaphore_signal(
            barrier, inc=1, device_id={"rad": rad, "az": lax.rem(az + d, n_az)}, device_id_type=MESH
        )
    inside = jnp.logical_and(has[-1], has[1])
    near = jnp.where(inside, 8, 5 if n_rad > 1 else 2)
    pl.semaphore_wait(barrier, near + len(farther))

    def radial(step):
        return pltpu.make_async_remote_copy(
            src_ref=block_ref,
            dst_ref=up_ref if step < 0 else low_ref,
            send_sem=send_sem.at[0 if step < 0 else 1],
            recv_sem=recv_sem.at[0 if step < 0 else 1],
            device_id={"rad": rad + step, "az": az},
            device_id_type=MESH,
        )

    def edge(step, side):
        slot = side * 3 + 1 - step
        return pltpu.make_async_remote_copy(
            src_ref=pack_ref.at[side],
            dst_ref=edge_ref.at[slot],
            send_sem=send_sem.at[2 + slot],
            recv_sem=recv_sem.at[2 + slot],
            device_id={"rad": rad + step, "az": left if side == 0 else right},
            device_id_type=MESH,
        )

    for step in (-1, 1):
        when(step, lambda step=step: radial(step).start())
    for side in (0, 1):
        pack_edges(block_ref, pack_ref, side)
        for step in (0, -1, 1):
            when(step, lambda step=step, side=side: edge(step, side).start())
    for side in (0, 1):
        edge(0, side).wait_recv()
    if between is not None:
        between()
    for side in (0, 1):
        edge(0, side).wait_send()
        for step in (-1, 1):
            when(step, lambda step=step, side=side: edge(step, side).wait_send())
            when(-step, lambda step=step, side=side: edge(step, side).wait_recv())
    for step in (-1, 1):
        when(step, lambda step=step: radial(step).wait_send())
        when(-step, lambda step=step: radial(step).wait_recv())


def interface(before, centre, follow, beyond):
    value = 7.0 / 12.0 * (centre + follow) - 1.0 / 12.0 * (before + beyond)
    return jnp.clip(value, jnp.minimum(centre, follow), jnp.maximum(centre, follow))


def limited(u, left, right):
    flat = (right - u) * (u - left) <= 0.0
    spread = right - left
    middle = u - 0.5 * (left + right)
    product = spread * middle
    sixth = spread * spread * (1.0 / 6.0)
    triple = 3.0 * u
    new_left = jnp.where(flat, u, jnp.where(product > sixth, triple - 2.0 * right, left))
    new_right = jnp.where(flat, u, jnp.where(product < -sixth, triple - 2.0 * left, right))
    return new_left, new_right


def hllc(left, right, normal):
    gas_left, gas_right = ADIABATIC * left[4], ADIABATIC * right[4]
    sound_left = gas_left * lax.rsqrt(gas_left * left[0])
    sound_right = gas_right * lax.rsqrt(gas_right * right[0])
    u_left, u_right = left[normal], right[normal]
    slow = jnp.minimum(u_left - sound_left, u_right - sound_right)
    fast = jnp.maximum(u_left + sound_left, u_right + sound_right)
    mass_left = left[0] * (u_left - slow)
    mass_right = right[0] * (fast - u_right)
    contact = (mass_left * u_left + mass_right * u_right + left[4] - right[4]) / (
        mass_left + mass_right
    )
    supersonic = slow >= 0.0
    from_left = jnp.logical_or(supersonic, contact >= 0.0)
    rho, v1, v2, v3, p = [jnp.where(from_left, a, b) for a, b in zip(left, right)]
    speeds = (None, v1, v2, v3)
    u = speeds[normal]
    wave = jnp.where(from_left, slow, fast)
    star = jnp.logical_and(slow < 0.0, jnp.logical_or(from_left, fast > 0.0))
    energy = p * (1.0 / (ADIABATIC - 1.0)) + 0.5 * rho * (v1 * v1 + v2 * v2 + v3 * v3)
    momentum = rho * u
    relative = wave - u
    mass = rho * relative
    inverse = 1.0 / (wave - contact)
    factor = mass * inverse
    star_energy = inverse * (relative * energy + (contact - u) * (mass * contact + p))
    flux_mass = momentum + jnp.where(star, wave * (factor - rho), 0.0)
    flux_normal = momentum * u + p + jnp.where(star, wave * (factor * contact - momentum), 0.0)
    flux_energy = (energy + p) * u + jnp.where(star, wave * (star_energy - energy), 0.0)
    out = [flux_mass, None, None, None, flux_energy]
    for axis in (1, 2, 3):
        out[axis] = flux_normal if axis == normal else speeds[axis] * flux_mass
    return out


def conserved_of(w):
    energy = w[4] * (1.0 / (ADIABATIC - 1.0)) + 0.5 * w[0] * (
        w[1] * w[1] + w[2] * w[2] + w[3] * w[3]
    )
    return [w[0], w[0] * w[1], w[0] * w[2], w[0] * w[3], energy]


def primitive_of(u):
    inverse = 1.0 / u[0]
    v = [inverse * u[k] for k in (1, 2, 3)]
    squared = v[0] * v[0] + v[1] * v[1] + v[2] * v[2]
    return [u[0]] + v + [(ADIABATIC - 1.0) * (u[4] - 0.5 * u[0] * squared)]


def rolled(x, amount, axis):
    return pltpu.roll(x, amount % x.shape[axis], axis)


def azimuth_difference(w):
    lows, highs = [], []
    for u in w:
        edge = interface(rolled(u, 1, 1), u, rolled(u, -1, 1), rolled(u, -2, 1))
        low, high = limited(u, rolled(edge, 1, 1), edge)
        lows.append(low)
        highs.append(rolled(high, 1, 1))
    flux = hllc(highs, lows, 3)
    return [rolled(f, -1, 1) - f for f in flux]


def polar_difference(w):
    count = w[0].shape[0]
    place = lax.broadcasted_iota(jnp.int32, w[0].shape, 0)
    first, last = place == 0, place == count - 1
    beyond_last = place >= count - 2
    lows, highs = [], []
    for u in w:
        before = jnp.where(first, u, rolled(u, 1, 0))
        follow = jnp.where(last, u, rolled(u, -1, 0))
        beyond = jnp.where(beyond_last, jnp.where(last, u, follow), rolled(u, -2, 0))
        edge = interface(before, u, follow, beyond)
        low, high = limited(u, jnp.where(first, u, rolled(edge, 1, 0)), edge)
        lows.append(low)
        highs.append(jnp.where(first, u, rolled(high, 1, 0)))
    flux = hllc(highs, lows, 2)
    rho, v1, v2, v3, p = w
    momentum = rho * v2
    energy = conserved_of(w)[4]
    outer = [momentum, momentum * v1, momentum * v2 + p, momentum * v3, (energy + p) * v2]
    return [jnp.where(last, o, rolled(f, -1, 0)) - f for f, o in zip(flux, outer)]


def row_of(ref, row, width):
    return [ref[c, row, :, :width] for c in range(5)]


def radial_start(src, cell, width, keep):
    w = [row_of(src, cell + k, width) for k in (-2, -1, 0, 1, 2)]
    for c in range(5):
        below = interface(*(w[k][c] for k in (0, 1, 2, 3)))
        above = interface(*(w[k][c] for k in (1, 2, 3, 4)))
        keep[0, c, :, :width] = above
        keep[1, c, :, :width] = limited(w[2][c], below, above)[1]


def radial_face(src, cell, width, keep):
    w = [row_of(src, cell + k, width) for k in (0, 1, 2, 3)]
    highs, lows = [], []
    for c in range(5):
        below = keep[0, c, :, :width]
        above = interface(*(w[k][c] for k in (0, 1, 2, 3)))
        low, high = limited(w[1][c], below, above)
        highs.append(keep[1, c, :, :width])
        lows.append(low)
        keep[0, c, :, :width] = above
        keep[1, c, :, :width] = high
    return hllc(highs, lows, 1)


def stage_begin(src, cell, width, keep):
    radial_start(src, cell - 1, width, keep)
    flux = radial_face(src, cell - 1, width, keep)
    for c in range(5):
        keep[2, c, :, :width] = flux[c]


def cross_change(src, cell, width, courant):
    total = [COURANT_POLAR * d for d in polar_difference(row_of(src, cell, width))]
    for c, d in enumerate(azimuth_difference(row_of(src, cell, src.shape[3]))):
        total[c] += courant * d[:, :width]
    return total


def radial_change(src, cell, width, keep):
    upper = radial_face(src, cell, width, keep)
    total = []
    for c in range(5):
        total.append(COURANT_RADIAL * (upper[c] - keep[2, c, :, :width]))
        keep[2, c, :, :width] = upper[c]
    return total


def courant_of(row, rows, n_rad):
    index = jnp.full((1, 1), lax.axis_index("rad") * rows + row, jnp.int32).astype(jnp.float32)
    return COURANT_AZIMUTH / (1.0 + (index + 0.5) / (rows * n_rad))


def unpacked(edge_ref, which, plane):
    lane = lax.broadcasted_iota(jnp.int32, edge_ref.shape[2:], 1)
    tile, slot = plane // PER_TILE, plane % PER_TILE
    after = rolled(edge_ref[which, tile], -slot * SLOT, 1)
    before = rolled(edge_ref[3 + which, tile], -(slot * SLOT + SLOT), 1)
    return jnp.where(lane < SLOT, after, before)


def own_rows(n_rad, block_ref, edge_ref, wide_ref, cross_ref):
    comps, rows, polar, cells = block_ref.shape
    for c in range(comps):
        for r in range(rows):
            wide_ref[c, DEEP + r, :, :cells] = block_ref[c, r]
            wide_ref[c, DEEP + r, :, cells:] = unpacked(edge_ref, 1, c * rows + r)

    def row(r, carry):
        change = cross_change(wide_ref, DEEP + r, cells + LANES, courant_of(r, rows, n_rad))
        for c in range(comps):
            cross_ref[c, r] = change[c]
        return carry

    lax.fori_loop(0, rows, row, 0)


def stage_kernel(
    n_rad, block_ref, low_ref, up_ref, edge_ref, out_ref, wide_ref, first_ref, half_ref, keep1, keep2,
    cross_ref, after=None, own_done=False,
):
    comps, rows, polar, cells = block_ref.shape
    rad = lax.axis_index("rad")
    if not own_done:
        own_rows(n_rad, block_ref, edge_ref, wide_ref, cross_ref)

    is_first, is_last = rad == 0, rad == n_rad - 1
    for c in range(comps):
        bottom, top = wide_ref[c, DEEP, :, cells:], wide_ref[c, DEEP + rows - 1, :, cells:]
        for r in range(DEEP):
            below, above = r, DEEP + rows + r
            low, up = c * rows + rows - DEEP + r, c * rows + r
            wide_ref[c, below, :, :cells] = jnp.where(
                is_first, block_ref[c, 0], low_ref[c, rows - DEEP + r]
            )
            wide_ref[c, above, :, :cells] = jnp.where(is_last, block_ref[c, rows - 1], up_ref[c, r])
            wide_ref[c, below, :, cells:] = jnp.where(is_first, bottom, unpacked(edge_ref, 0, low))
            wide_ref[c, above, :, cells:] = jnp.where(is_last, top, unpacked(edge_ref, 2, up))

    width = cells + LANES
    stage_begin(wide_ref, 3, width, keep1)

    def first_row(k, own, above=False):
        if own:
            cross = [cross_ref[c, k - 3] for c in range(comps)]
        else:
            cross = cross_change(wide_ref, k + 3, width, courant_of(k - 3, rows, n_rad))
        radial = radial_change(wide_ref, k + 3, width, keep1)
        start = conserved_of(row_of(wide_ref, k + 3, width))
        new = [a - (b + d) for a, b, d in zip(start, radial, cross)]
        w = primitive_of(new)
        for c in range(comps):
            first_ref[c, k, :, :] = (
                jnp.where(is_last, first_ref[c, rows + 2], w[c]) if above else w[c]
            )
            half_ref[c, k, :, :] = (0.5 * start[c] + 0.5 * new[c])[:, :cells]

    for begin, end, own in ((0, 3, False), (3, 7, True)):
        lax.fori_loop(begin, end, lambda k, carry, own=own: (first_row(k, own), carry)[1], 0)

    @pl.when(is_first)
    def _():
        for r in range(3):
            first_ref[:, r] = first_ref[:, 3]

    for spare in range(rows * comps, out_ref.shape[0]):
        out_ref[spare] = jnp.zeros((polar, cells), jnp.float32)
    stage_begin(first_ref, 3, cells, keep2)

    def second_row(i, carry):
        radial = radial_change(first_ref, i + 3, cells, keep2)
        cross = cross_change(first_ref, i + 3, cells, courant_of(i, rows, n_rad))
        change = [a + b for a, b in zip(radial, cross)]
        w = primitive_of([half_ref[c, i + 3] - 0.5 * change[c] for c in range(comps)])
        for c in range(comps):
            out_ref[i * comps + c] = w[c]
        if after is not None:
            after(i)
        return carry

    def both(i, carry, above):
        second_row(i, 0)
        first_row(i + 7, not above, above)
        return carry

    lax.fori_loop(0, rows - 4, functools.partial(both, above=False), 0)
    lax.fori_loop(rows - 4, rows - 1, functools.partial(both, above=True), 0)
    second_row(jnp.int32(rows - 1), 0)


def turn_kernel(n_az, planes_ref, shifts_ref, out_ref, far_ref, send_sem, recv_sem):
    rad, az = lax.axis_index("rad"), lax.axis_index("az")
    comps, rows, polar, cells = out_ref.shape
    barrier = pltpu.get_barrier_semaphore()
    for d in range(1, REACH + 1):
        for column in (lax.rem(az + d, n_az), lax.rem(az + n_az - d, n_az)):
            pl.semaphore_signal(
                barrier, inc=1, device_id={"rad": rad, "az": column}, device_id_type=MESH
            )
    pl.semaphore_wait(barrier, 2 * REACH)

    def send(d):
        return pltpu.make_async_remote_copy(
            src_ref=planes_ref,
            dst_ref=far_ref.at[d - 1],
            send_sem=send_sem.at[d - 1],
            recv_sem=recv_sem.at[d - 1],
            device_id={"rad": rad, "az": lax.rem(az + d, n_az)},
            device_id_type=MESH,
        )

    for d in range(1, REACH + 1):
        send(d).start()
    for d in range(1, REACH + 1):
        send(d).wait()
    lane = lax.broadcasted_iota(jnp.int32, (polar, cells), 1)
    for i in range(rows):
        amount = shifts_ref[i]
        quotient = amount // cells
        rest = amount - quotient * cells
        for c in range(comps):
            blocks = [planes_ref[i * comps + c]] + [far_ref[d, i * comps + c] for d in range(REACH)]
            near, far = blocks[0], blocks[1]
            for d in range(1, REACH + 1):
                near = jnp.where(quotient == d, blocks[d], near)
                if d < REACH:
                    far = jnp.where(quotient == d, blocks[d + 1], far)
            out_ref[c, i] = pltpu.roll(jnp.where(lane >= cells - rest, far, near), rest, 1)


def quarter_turn_kernel(
    n_rad, n_az, block_ref, shifts_ref, out_ref, low_ref, up_ref, edge_ref, pack_ref, halo_send,
    halo_recv, far_ref, turned_ref, back_ref, send_sem, recv_sem, planes_ref, *stage_refs
):
    rad, az = lax.axis_index("rad"), lax.axis_index("az")
    comps, rows, polar, cells = out_ref.shape
    share = planes_ref.shape[0] // n_az
    halo_kernel(
        n_rad, n_az, block_ref, low_ref, up_ref, edge_ref, pack_ref, halo_send, halo_recv,
        tuple(range(2, n_az - 1)),
        lambda: own_rows(n_rad, block_ref, edge_ref, stage_refs[0], stage_refs[-1]),
    )

    def gather(d):
        owner = lax.rem(az + d, n_az)
        return pltpu.make_async_remote_copy(
            src_ref=planes_ref.at[pl.ds(owner * share, share)],
            dst_ref=far_ref.at[d - 1],
            send_sem=send_sem.at[d - 1],
            recv_sem=recv_sem.at[d - 1],
            device_id={"rad": rad, "az": owner},
            device_id_type=MESH,
        )

    def home(g):
        return pltpu.make_async_remote_copy(
            src_ref=turned_ref.at[g],
            dst_ref=back_ref.at[pl.ds(az * share, share)],
            send_sem=send_sem.at[n_az - 2 + g],
            recv_sem=recv_sem.at[n_az - 2 + g],
            device_id={"rad": rad, "az": lax.rem(az + g, n_az)},
            device_id_type=MESH,
        )

    def after(i):
        for owner in range(n_az):
            last = (min((owner + 1) * share, rows * comps) - 1) // comps
            d = lax.rem(owner - az + n_az, n_az)

            @pl.when(jnp.logical_and(i == last, az != owner))
            def _(owner=owner, d=d):
                pltpu.make_async_remote_copy(
                    src_ref=planes_ref.at[pl.ds(owner * share, share)],
                    dst_ref=far_ref.at[d - 1],
                    send_sem=send_sem.at[d - 1],
                    recv_sem=recv_sem.at[d - 1],
                    device_id={"rad": rad, "az": owner},
                    device_id_type=MESH,
                ).start()

    stage_kernel(
        n_rad, block_ref, low_ref, up_ref, edge_ref, planes_ref, *stage_refs, after=after,
        own_done=True,
    )
    for d in range(1, n_az):
        gather(d).wait()
    lane = lax.broadcasted_iota(jnp.int32, (polar, cells), 1)
    for k in range(share):
        row = jnp.minimum((az * share + k) // comps, rows - 1)
        amount = shifts_ref[row]
        quotient = amount // cells
        rest = amount - quotient * cells
        blocks = [planes_ref[az * share + k]] + [far_ref[d, k] for d in range(n_az - 1)]
        blocks = [pltpu.roll(b, rest, 1) for b in blocks]
        ahead = blocks
        for q in range(1, n_az):
            ahead = [
                jnp.where(quotient == q, blocks[(q + j) % n_az], a) for j, a in enumerate(ahead)
            ]
        for g in range(n_az):
            turned = jnp.where(lane < rest, ahead[(1 - g) % n_az], ahead[-g % n_az])
            if g:
                turned_ref[g, k] = turned
            else:
                back_ref[az * share + k] = turned
    for g in range(1, n_az):
        home(g).start()
    for g in range(1, n_az):
        home(g).wait_send()
        sender = lax.rem(az + n_az - g, n_az)
        pltpu.make_async_remote_copy(
            src_ref=turned_ref.at[g],
            dst_ref=back_ref.at[pl.ds(sender * share, share)],
            send_sem=send_sem.at[n_az - 2 + g],
            recv_sem=recv_sem.at[n_az - 2 + g],
            device_id={"rad": rad, "az": lax.rem(az + g, n_az)},
            device_id_type=MESH,
        ).wait_recv()
    for i in range(rows):
        for c in range(comps):
            out_ref[c, i] = back_ref[i * comps + c]


def on_device(n_rad, n_az, fields, shifts):
    comps, rows, polar, cells = fields.shape
    vmem = pl.BlockSpec(memory_space=pltpu.VMEM)
    tiles = -(-comps * rows // PER_TILE)
    f32 = functools.partial(jax.ShapeDtypeStruct, dtype=jnp.float32)
    width = cells + LANES
    count = -(-rows * comps // 8) * 8
    stage_scratch = [
        pltpu.VMEM((comps, rows + 2 * DEEP, polar, width), jnp.float32),
        pltpu.VMEM((comps, rows + DEEP, polar, width), jnp.float32),
        pltpu.VMEM((comps, rows + DEEP, polar, cells), jnp.float32),
        pltpu.VMEM((3, comps, polar, width), jnp.float32),
        pltpu.VMEM((3, comps, polar, width), jnp.float32),
        pltpu.VMEM((comps, rows, polar, width), jnp.float32),
    ]
    if n_az == 4:
        share = count // n_az
        return pl.pallas_call(
            functools.partial(quarter_turn_kernel, n_rad, n_az),
            out_shape=f32(fields.shape),
            in_specs=[vmem, pl.BlockSpec(memory_space=pltpu.SMEM)],
            out_specs=vmem,
            scratch_shapes=[
                pltpu.VMEM(fields.shape, jnp.float32),
                pltpu.VMEM(fields.shape, jnp.float32),
                pltpu.VMEM((6, tiles, polar, LANES), jnp.float32),
                pltpu.VMEM((2, tiles, polar, LANES), jnp.float32),
                pltpu.SemaphoreType.DMA((8,)),
                pltpu.SemaphoreType.DMA((8,)),
                pltpu.VMEM((n_az - 1, share, polar, cells), jnp.float32),
                pltpu.VMEM((n_az, share, polar, cells), jnp.float32),
                pltpu.VMEM((count, polar, cells), jnp.float32),
                pltpu.SemaphoreType.DMA((2 * n_az - 2,)),
                pltpu.SemaphoreType.DMA((2 * n_az - 2,)),
                pltpu.VMEM((count, polar, cells), jnp.float32),
                *stage_scratch,
            ],
            compiler_params=pltpu.CompilerParams(
                collective_id=1, has_side_effects=True, vmem_limit_bytes=32 * 1024 * 1024
            ),
            name="whole_step",
        )(fields, shifts)
    low, up, edges = pl.pallas_call(
        functools.partial(halo_kernel, n_rad, n_az),
        out_shape=(f32(fields.shape), f32(fields.shape), f32((6, tiles, polar, LANES))),
        in_specs=[vmem],
        out_specs=(vmem, vmem, vmem),
        scratch_shapes=[
            pltpu.VMEM((2, tiles, polar, LANES), jnp.float32),
            pltpu.SemaphoreType.DMA((8,)),
            pltpu.SemaphoreType.DMA((8,)),
        ],
        compiler_params=pltpu.CompilerParams(collective_id=0, has_side_effects=True),
        name="halo",
    )(fields)
    planes = pl.pallas_call(
        functools.partial(stage_kernel, n_rad),
        out_shape=f32((count, polar, cells)),
        in_specs=[vmem] * 4,
        out_specs=vmem,
        scratch_shapes=stage_scratch,
        compiler_params=pltpu.CompilerParams(vmem_limit_bytes=32 * 1024 * 1024),
        name="stages",
    )(fields, low, up, edges)
    return pl.pallas_call(
        functools.partial(turn_kernel, n_az),
        out_shape=f32(fields.shape),
        in_specs=[vmem, pl.BlockSpec(memory_space=pltpu.SMEM)],
        out_specs=vmem,
        scratch_shapes=[
            pltpu.VMEM((REACH, count, polar, cells), jnp.float32),
            pltpu.SemaphoreType.DMA((REACH,)),
            pltpu.SemaphoreType.DMA((REACH,)),
        ],
        compiler_params=pltpu.CompilerParams(collective_id=1, has_side_effects=True),
        name="turn",
    )(planes, shifts)


def solution(mesh):
    return jax.shard_map(
        functools.partial(on_device, mesh.shape["rad"], mesh.shape["az"]),
        mesh=mesh,
        in_specs=(P(None, "rad", None, "az"), P("rad")),
        out_specs=P(None, "rad", None, "az"),
        check_vma=False,
    )
```
